512 devices in a mesh: dp: 8 (over y_lo, x), resp: 32 (over y_hi, z), tensor: 2 (over core).
Axes of the slice: x: 4, y: 8 (y_hi: 4, y_lo: 2; y = y_hi * 2 + y_lo), z: 8, core: 2. Of those that a mesh axis runs over, the one named last changes fastest.
Arguments:
- query_raw: bfloat16 [8, 32, 128, 4096], P('dp', 'resp', None, 'tensor'), may hold values from -6 to 6
- response_key_input: bfloat16 [8, 32, 128, 512], P('dp', 'resp', None, 'tensor'), may hold values from -6 to 6
- response_value_input: bfloat16 [8, 32, 128, 512], P('dp', 'resp', None, 'tensor'), may hold values from -6 to 6
- prompt_key_input: bfloat16 [8, 256, 512], P('dp', 'resp', 'tensor'), may hold values from -6 to 6
- prompt_value_input: bfloat16 [8, 256, 512], P('dp', 'resp', 'tensor'), may hold values from -6 to 6
- query_gain: float32 [128], replicated, may hold values from 0.1 to 1.9
- key_gain: float32 [128], replicated, may hold values from 0.1 to 1.9
- grad_out: bfloat16 [8, 32, 128, 4096], P('dp', 'resp', None, 'tensor'), may hold values from -12 to 12
- rewards: float32 [8, 32], P('dp', 'resp'), may hold values from -12 to 12
- resp_len: int32 [8, 32], P('dp', 'resp'), may hold values from 1 to 128, as said below
- prompt_len: int32 [8], P('dp'), may hold values from 64 to 256, as said below
Outputs:
- grad_query: bfloat16 [8, 32, 128, 4096], P('dp', 'resp', None, 'tensor')
- grad_key: bfloat16 [8, 32, 128, 512], P('dp', 'resp', None, 'tensor')
- grad_value: bfloat16 [8, 32, 128, 512], P('dp', 'resp', None, 'tensor')
- grad_prefix_key: float32 [8, 256, 512], P('dp', 'resp', 'tensor')
- grad_prefix_value: float32 [8, 256, 512], P('dp', 'resp', 'tensor')
- grad_query_gain: float32 [128], replicated
- grad_key_gain: float32 [128], replicated
The draws below stay inside these ranges and needn't reach their ends.
Inputs may be any that keep to these rules, and one draw needn't show every extreme that they name: `resp_len`: each response has 1 to 128 valid tokens, and in every draw some response has exactly 128. `prompt_len`: each prompt has 64 to 256 valid tokens, and in every draw some prompt has exactly 256.
All inputs are finite; a program needn't handle non-finite values.
Results may differ from the reference program's by a relative error of at most 0.0078.
Values may be sent and summed in bfloat16 or wider, within the bound.
No kernel may reach another device: no remote copies, remote signals or barrier semaphores. Data moves between devices by JAX's collectives and lax.ppermute only.
A program may use at most 64 MiB of HBM per device.

```python
import jax
import jax.numpy as jnp
from jax import lax

QUERY_HEAD_COUNT = 32
KEY_VALUE_HEADS = 4
HEAD_SIZE = 128
RESPONSE_SLOTS = 128
PROMPT_SLOTS = 256
PROMPT_GROUPS = 8
RESPONSE_COUNT = 32


def draw_rewards(key, part):
    key = jax.random.fold_in(key, 11)
    ramp_scale = 1.0 + 2.0 * jnp.arange(RESPONSE_COUNT, dtype=jnp.float32) / (RESPONSE_COUNT - 1)
    base_draw = jnp.clip(jax.random.normal(key, (PROMPT_GROUPS, RESPONSE_COUNT), jnp.float32), -4.0, 4.0)
    return base_draw * ramp_scale[None, :]


def draw_resp_len(key, part):
    key = jax.random.fold_in(key, 23)
    first_key, second_key = jax.random.split(key)
    lengths = jax.random.randint(first_key, (PROMPT_GROUPS * RESPONSE_COUNT,), 1, RESPONSE_SLOTS + 1)
    chosen = jax.random.randint(second_key, (), 0, PROMPT_GROUPS * RESPONSE_COUNT)
    lengths = jnp.where(jnp.arange(PROMPT_GROUPS * RESPONSE_COUNT) == chosen, RESPONSE_SLOTS, lengths)
    return lengths.reshape(PROMPT_GROUPS, RESPONSE_COUNT).astype(jnp.int32)


def draw_prompt_len(key, part):
    key = jax.random.fold_in(key, 37)
    first_key, second_key = jax.random.split(key)
    lengths = jax.random.randint(first_key, (PROMPT_GROUPS,), PROMPT_SLOTS // 4, PROMPT_SLOTS + 1)
    chosen = jax.random.randint(second_key, (), 0, PROMPT_GROUPS)
    lengths = jnp.where(jnp.arange(PROMPT_GROUPS) == chosen, PROMPT_SLOTS, lengths)
    return lengths.astype(jnp.int32)


def steps_of(rng, shape, shards, low, largest):
    factor_of = 1.0
    for dim, parts in shards:
        heights = jax.random.uniform(jax.random.fold_in(jax.random.fold_in(rng, 6), dim), (parts,), jnp.float32, low / len(shards), largest / len(shards))
        factor_of = factor_of * jnp.repeat(jnp.exp(heights), shape[dim] // parts).reshape((-1,) + (1,) * (len(shape) - 1 - dim))
    return factor_of


def bell_draw(stream_key, shape, scale, limit, shards=(), kind=jnp.bfloat16):
    drawn = jax.random.normal(stream_key, shape, jnp.float32) * scale
    if len(shards) > 0:
        drawn = steps_of(stream_key, shape, shards, -0.22, 0.18) * drawn
    return jnp.clip(drawn, min=-limit, max=limit).astype(kind)


def setup_inputs(seed: int = 0) -> dict:
    key_list = jax.random.split(jax.random.key(seed), 12)
    return {
        "query_raw": bell_draw(key_list[0], (PROMPT_GROUPS, RESPONSE_COUNT, RESPONSE_SLOTS, QUERY_HEAD_COUNT * HEAD_SIZE), 1.0, 6.0, ((0, 8), (1, 32), (3, 2))),
        "response_key_input": bell_draw(key_list[1], (PROMPT_GROUPS, RESPONSE_COUNT, RESPONSE_SLOTS, KEY_VALUE_HEADS * HEAD_SIZE), 1.0, 6.0, ((0, 8), (1, 32), (3, 2))),
        "response_value_input": bell_draw(key_list[2], (PROMPT_GROUPS, RESPONSE_COUNT, RESPONSE_SLOTS, KEY_VALUE_HEADS * HEAD_SIZE), 1.0, 6.0, ((0, 8), (1, 32), (3, 2))),
        "prompt_key_input": bell_draw(key_list[3], (PROMPT_GROUPS, PROMPT_SLOTS, KEY_VALUE_HEADS * HEAD_SIZE), 1.0, 6.0, ((0, 8), (1, 32), (2, 2))),
        "prompt_value_input": bell_draw(key_list[4], (PROMPT_GROUPS, PROMPT_SLOTS, KEY_VALUE_HEADS * HEAD_SIZE), 1.0, 6.0, ((0, 8), (1, 32), (2, 2))),
        "query_gain": jnp.clip(1.0 + 0.18 * jax.random.normal(key_list[5], (HEAD_SIZE,), jnp.float32), 0.1, 1.9),
        "key_gain": jnp.clip(1.0 + 0.18 * jax.random.normal(key_list[6], (HEAD_SIZE,), jnp.float32), 0.1, 1.9),
        "grad_out": bell_draw(key_list[7], (PROMPT_GROUPS, RESPONSE_COUNT, RESPONSE_SLOTS, QUERY_HEAD_COUNT * HEAD_SIZE), 2.0, 12.0, ((0, 8), (1, 32), (3, 2))),
        "rewards": draw_rewards(jax.random.fold_in(key_list[11], 71), 0),
        "resp_len": draw_resp_len(jax.random.fold_in(key_list[11], 71), 0),
        "prompt_len": draw_prompt_len(jax.random.fold_in(key_list[11], 71), 0),
    }


EPSILON = 1e-06
THETA = 1000000.0

def rotate(vectors):
    half_width = vectors.shape[-1] // 2
    return jnp.concatenate([-vectors[..., half_width:], vectors[..., :half_width]], axis=-1)

def rotate_back(vectors):
    half_width = vectors.shape[-1] // 2
    return jnp.concatenate([vectors[..., half_width:], -vectors[..., :half_width]], axis=-1)

def tables(positions, head_dimension):
    half_width = head_dimension // 2
    inv_freq = THETA ** (-(jnp.arange(half_width, dtype=jnp.float32) * 2.0) / head_dimension)
    angles = positions.astype(jnp.float32)[:, None] * inv_freq[None, :]
    angles = jnp.concatenate([angles, angles], axis=1)
    return (jnp.cos(angles)[:, None, :], jnp.sin(angles)[:, None, :])

def norm_rope(raw_rows, gain_vec, positions, head_dimension):
    row_count = raw_rows.shape[0]
    raw_f32 = raw_rows.astype(jnp.float32).reshape(row_count, -1, head_dimension)
    inverse = lax.rsqrt(lax.optimization_barrier(jnp.mean(raw_f32 * raw_f32, axis=-1, keepdims=True)) + EPSILON)
    unit_vec = raw_f32 * inverse
    normed = unit_vec * gain_vec
    cos_table, sin_table = tables(positions, head_dimension)
    rotated = normed * cos_table + rotate(normed) * sin_table
    return (rotated.astype(jnp.bfloat16), unit_vec, inverse, cos_table, sin_table)

def norm_rope_back(grad_in, unit_vec, inverse, gain_vec, cos_table, sin_table):
    normed_grad = grad_in * cos_table + rotate_back(grad_in * sin_table)
    gain_term = lax.optimization_barrier(jnp.sum(normed_grad * unit_vec, axis=(0, 1)))
    unit_grad = normed_grad * gain_vec
    raw_grad = inverse * (unit_grad - unit_vec * lax.optimization_barrier(jnp.mean(unit_grad * unit_vec, axis=-1, keepdims=True)))
    return (raw_grad, gain_term)

def heads_per_key(query_matrix, joined_keys, value_matrix, output_gradient, starting_position, token_numbers):
    column_ids = jnp.arange(PROMPT_SLOTS + RESPONSE_SLOTS, dtype=jnp.int32)
    allowed = jnp.where(column_ids[None, :] < PROMPT_SLOTS, column_ids[None, :] < starting_position, column_ids[None, :] - PROMPT_SLOTS <= token_numbers[:, None])
    score_scale = query_matrix.shape[-1] ** (-0.5)

    def one_head(accum, inputs):
        query_rows, grad_rows = inputs
        score = jnp.dot(query_rows, joined_keys.T, preferred_element_type=jnp.float32) * score_scale
        expo_score = jnp.where(allowed, jnp.exp(score), 0.0)
        prob_f32 = expo_score / lax.optimization_barrier(jnp.sum(expo_score, axis=1, keepdims=True))
        prob_low = prob_f32.astype(jnp.bfloat16)
        dprob_f32 = jnp.dot(grad_rows, value_matrix.T, preferred_element_type=jnp.float32)
        delta_row = lax.optimization_barrier(jnp.sum(prob_f32 * dprob_f32, axis=1, keepdims=True))
        dscore = (prob_f32 * (dprob_f32 - delta_row) * score_scale).astype(jnp.bfloat16)
        query_gradient_out = jnp.dot(dscore, joined_keys, preferred_element_type=jnp.float32)
        key_gradient_full = accum[0] + jnp.dot(dscore.T, query_rows, preferred_element_type=jnp.float32)
        value_gradient_out = accum[1] + jnp.dot(prob_low.T, grad_rows, preferred_element_type=jnp.float32)
        return ((key_gradient_full, value_gradient_out), query_gradient_out)
    zero_acc = jnp.zeros(joined_keys.shape, jnp.float32)
    (key_gradient_full, value_gradient_out), query_gradient_out = lax.scan(one_head, (zero_acc, zero_acc), (query_matrix, output_gradient))
    return (query_gradient_out, key_gradient_full, value_gradient_out)

def reference(query_raw, response_key_input, response_value_input, prompt_key_input, prompt_value_input, query_gain, key_gain, grad_out, rewards, resp_len, prompt_len):
    head_dimension = HEAD_SIZE
    responses_per_group = QUERY_HEAD_COUNT // KEY_VALUE_HEADS
    token_numbers = jnp.arange(RESPONSE_SLOTS, dtype=jnp.int32)
    advantage = rewards - lax.optimization_barrier(jnp.sum(rewards, axis=1, keepdims=True)) / RESPONSE_COUNT

    def one_group(operands):
        query_g, key_g, value_g, pre_key, prompt_value_rows, grad_g, adv_g, len_g, starting_position = operands
        pre_rot, pre_unit, pre_inv, pre_cos, pre_sin = norm_rope(pre_key, key_gain, jnp.arange(PROMPT_SLOTS, dtype=jnp.int32), head_dimension)
        positions = starting_position + token_numbers

        def one_response(accum, inner):
            query_r, key_r, response_value_rows, grad_r, adv_r, len_r = inner
            rotated_query_rows, query_unit, query_inv, query_cos, query_sin = norm_rope(query_r, query_gain, positions, head_dimension)
            key_rot, key_unit, key_inv, key_cos, key_sin = norm_rope(key_r, key_gain, positions, head_dimension)
            output_gradient = jnp.where((token_numbers < len_r)[:, None], grad_r.astype(jnp.float32) * adv_r, 0.0).astype(jnp.bfloat16)
            joined_keys = jnp.concatenate([pre_rot, key_rot], axis=0).transpose(1, 0, 2)
            value_matrix = jnp.concatenate([prompt_value_rows.reshape(PROMPT_SLOTS, KEY_VALUE_HEADS, head_dimension), response_value_rows.reshape(RESPONSE_SLOTS, KEY_VALUE_HEADS, head_dimension)], axis=0).transpose(1, 0, 2)
            query_matrix = rotated_query_rows.reshape(RESPONSE_SLOTS, KEY_VALUE_HEADS, responses_per_group, head_dimension).transpose(1, 2, 0, 3)
            incoming_gradients = output_gradient.reshape(RESPONSE_SLOTS, KEY_VALUE_HEADS, responses_per_group, head_dimension).transpose(1, 2, 0, 3)
            query_gradient_out, key_gradient_full, value_gradient_out = lax.map(lambda input_operands: heads_per_key(input_operands[0], input_operands[1], input_operands[2], input_operands[3], starting_position, token_numbers), (query_matrix, joined_keys, incoming_gradients.reshape(KEY_VALUE_HEADS, responses_per_group, RESPONSE_SLOTS, head_dimension)[:, :, :, :] * 0 + incoming_gradients if False else value_matrix, incoming_gradients))
            dquery_rot = query_gradient_out.transpose(2, 0, 1, 3).reshape(RESPONSE_SLOTS, QUERY_HEAD_COUNT, head_dimension)
            response_query_gradient, query_contribution = norm_rope_back(dquery_rot, query_unit, query_inv, query_gain, query_cos, query_sin)
            dkey_local = key_gradient_full[:, PROMPT_SLOTS:].transpose(1, 0, 2)
            response_key_gradient, key_contribution = norm_rope_back(dkey_local, key_unit, key_inv, key_gain, key_cos, key_sin)
            response_value_gradient = value_gradient_out[:, PROMPT_SLOTS:].transpose(1, 0, 2).reshape(RESPONSE_SLOTS, KEY_VALUE_HEADS * head_dimension)
            new_accum = (accum[0] + key_gradient_full[:, :PROMPT_SLOTS].transpose(1, 0, 2), accum[1] + value_gradient_out[:, :PROMPT_SLOTS].transpose(1, 0, 2), accum[2] + query_contribution, accum[3] + key_contribution)
            output_list = (response_query_gradient.reshape(RESPONSE_SLOTS, QUERY_HEAD_COUNT * head_dimension).astype(jnp.bfloat16), response_key_gradient.reshape(RESPONSE_SLOTS, KEY_VALUE_HEADS * head_dimension).astype(jnp.bfloat16), response_value_gradient.astype(jnp.bfloat16))
            return (new_accum, output_list)
        empty_prompt_gradient = jnp.zeros((PROMPT_SLOTS, KEY_VALUE_HEADS, head_dimension), jnp.float32)
        zero_gain = jnp.zeros((head_dimension,), jnp.float32)
        (dkey_pre, prompt_value_gradient, query_contribution, key_contribution), (group_query_gradient, group_key_gradient, group_value_gradient) = lax.scan(one_response, (empty_prompt_gradient, empty_prompt_gradient, zero_gain, zero_gain), (query_g, key_g, value_g, grad_g, adv_g, len_g))
        prompt_key_gradient, prompt_contribution = norm_rope_back(dkey_pre, pre_unit, pre_inv, key_gain, pre_cos, pre_sin)
        return (group_query_gradient, group_key_gradient, group_value_gradient, prompt_key_gradient.reshape(PROMPT_SLOTS, KEY_VALUE_HEADS * head_dimension), prompt_value_gradient.reshape(PROMPT_SLOTS, KEY_VALUE_HEADS * head_dimension), query_contribution, key_contribution + prompt_contribution)
    results = lax.map(one_group, (query_raw, response_key_input, response_value_input, prompt_key_input, prompt_value_input, grad_out, advantage, resp_len, prompt_len))
    grad_query, grad_key, grad_value, grad_prefix_key, grad_prefix_value, query_terms, key_terms = results
    grad_query_gain = lax.optimization_barrier(jnp.sum(query_terms, axis=0)) / (PROMPT_GROUPS * RESPONSE_COUNT)
    grad_key_gain = lax.optimization_barrier(jnp.sum(key_terms, axis=0)) / (PROMPT_GROUPS * RESPONSE_COUNT)
    return (grad_query, grad_key, grad_value, grad_prefix_key, grad_prefix_value, grad_query_gain, grad_key_gain)
```

```python
import jax
import jax.numpy as jnp
from jax import lax
from jax.sharding import PartitionSpec as P

EPSILON = 1e-06
THETA = 1000000.0


def rotate(vectors):
    half_width = vectors.shape[-1] // 2
    return jnp.concatenate([-vectors[..., half_width:], vectors[..., :half_width]], axis=-1)


def rotate_back(vectors):
    half_width = vectors.shape[-1] // 2
    return jnp.concatenate([vectors[..., half_width:], -vectors[..., :half_width]], axis=-1)


def tables(positions, head_dimension):
    half_width = head_dimension // 2
    inv_freq = THETA ** (-(jnp.arange(half_width, dtype=jnp.float32) * 2.0) / head_dimension)
    angles = positions.astype(jnp.float32)[:, None] * inv_freq[None, :]
    angles = jnp.concatenate([angles, angles], axis=1)
    return (jnp.cos(angles)[:, None, :], jnp.sin(angles)[:, None, :])


def norm_rope(raw_rows, gain_vec, positions, head_dimension):
    row_count = raw_rows.shape[0]
    raw_f32 = raw_rows.astype(jnp.float32).reshape(row_count, -1, head_dimension)
    inverse = lax.rsqrt(jnp.mean(raw_f32 * raw_f32, axis=-1, keepdims=True) + EPSILON)
    unit_vec = raw_f32 * inverse
    normed = unit_vec * gain_vec
    cos_table, sin_table = tables(positions, head_dimension)
    rotated = normed * cos_table + rotate(normed) * sin_table
    return (rotated.astype(jnp.bfloat16), unit_vec, inverse, cos_table, sin_table)


def norm_rope_back(grad_in, unit_vec, inverse, gain_vec, cos_table, sin_table):
    normed_grad = grad_in * cos_table + rotate_back(grad_in * sin_table)
    gain_term = jnp.sum(normed_grad * unit_vec, axis=(0, 1))
    unit_grad = normed_grad * gain_vec
    raw_grad = inverse * (
        unit_grad - unit_vec * jnp.mean(unit_grad * unit_vec, axis=-1, keepdims=True)
    )
    return (raw_grad, gain_term)


def kv_group(
    query_matrix, joined_keys, value_matrix, output_gradient, starting_position, prefix, length
):
    row_count, head_dimension = query_matrix.shape
    block_rows = min(512, row_count)
    block_count = row_count // block_rows
    score_scale = head_dimension ** (-0.5)
    column_ids = jnp.arange(joined_keys.shape[0], dtype=jnp.int32)
    query_blocks = query_matrix.reshape(block_count, block_rows, head_dimension)
    grad_blocks = output_gradient.reshape(block_count, block_rows, head_dimension)
    first_rows = jnp.arange(block_count, dtype=jnp.int32) * block_rows
    contract_rows = (((0,), (0,)), ((), ()))
    contract_last = (((1,), (1,)), ((), ()))

    def one_block(accum, inputs):
        query_rows, grad_rows, first_row = inputs
        token_numbers = (first_row + jnp.arange(block_rows, dtype=jnp.int32)) % length
        allowed = jnp.where(
            column_ids[None, :] < prefix,
            column_ids[None, :] < starting_position,
            column_ids[None, :] - prefix <= token_numbers[:, None],
        )
        score = (
            lax.dot_general(
                query_rows, joined_keys, contract_last, preferred_element_type=jnp.float32
            )
            * score_scale
        )
        expo_score = jnp.where(allowed, jnp.exp(score), 0.0)
        prob_f32 = expo_score / jnp.sum(expo_score, axis=1, keepdims=True)
        prob_low = prob_f32.astype(jnp.bfloat16)
        dprob_f32 = lax.dot_general(
            grad_rows, value_matrix, contract_last, preferred_element_type=jnp.float32
        )
        delta_row = jnp.sum(prob_f32 * dprob_f32, axis=1, keepdims=True)
        dscore = (prob_f32 * (dprob_f32 - delta_row) * score_scale).astype(jnp.bfloat16)
        query_gradient_out = jnp.dot(dscore, joined_keys, preferred_element_type=jnp.float32)
        saved = ()
        key_gradient_full = accum[0] + lax.dot_general(
            dscore, query_rows, contract_rows, preferred_element_type=jnp.float32
        )
        value_gradient_out = accum[1] + lax.dot_general(
            prob_low, grad_rows, contract_rows, preferred_element_type=jnp.float32
        )
        return ((key_gradient_full, value_gradient_out), (query_gradient_out, saved))

    acc_rows = joined_keys.shape[0]
    zero_acc = jnp.zeros((acc_rows, head_dimension), jnp.float32)
    (key_gradient_full, value_gradient_out), (query_gradient_out, saved) = lax.scan(
        one_block, (zero_acc, zero_acc), (query_blocks, grad_blocks, first_rows)
    )
    query_gradient_out = query_gradient_out.reshape(row_count, head_dimension)
    return (
        query_gradient_out,
        key_gradient_full[prefix:],
        value_gradient_out[prefix:],
        (key_gradient_full[:prefix], value_gradient_out[:prefix]),
    )


def split_terms(value, terms):
    found = []
    for _ in range(terms):
        term = lax.reduce_precision(value, 8, 7)
        found.append(term.astype(jnp.bfloat16))
        value = value - term
    return jnp.stack(found)


def local(
    query_raw,
    response_key_input,
    response_value_input,
    prompt_key_input,
    prompt_value_input,
    query_gain,
    key_gain,
    grad_out,
    rewards,
    resp_len,
    prompt_len,
):
    length = query_raw.shape[2]
    head_dimension = query_gain.shape[0]
    query_heads = query_raw.shape[3] // head_dimension
    kv_heads = response_key_input.shape[3] // head_dimension
    kv_cols = kv_heads * head_dimension
    responses_per_group = query_heads // kv_heads
    responses = lax.axis_size("resp")
    own_rows = prompt_key_input.shape[1]
    kv_width = 2 * kv_cols
    reward_cols = jnp.broadcast_to(split_terms(rewards[0, 0], 3), (own_rows, 3))
    reward_cols = jnp.pad(reward_cols, ((0, 0), (0, head_dimension - 3)))
    outgoing = jnp.concatenate([prompt_key_input[0], prompt_value_input[0], reward_cols], axis=1)
    arrived = lax.all_to_all(
        jnp.broadcast_to(outgoing[None], (responses,) + outgoing.shape), "resp", 0, 0
    )
    reward_all = jnp.sum(arrived[:, 0, kv_width : kv_width + 3].astype(jnp.float32), axis=1)
    advantage = rewards[0, 0] - jnp.sum(reward_all) / responses
    starting_position = prompt_len[0]
    token_numbers = jnp.arange(length, dtype=jnp.int32)
    positions = starting_position + token_numbers
    joined = arrived.reshape(1, responses * own_rows, kv_width + head_dimension)
    gathered_key, gathered_value = joined[:, :, :kv_cols], joined[:, :, kv_cols:kv_width]
    prefix = gathered_key.shape[1]
    pre_rot, pre_unit, pre_inv, pre_cos, pre_sin = norm_rope(
        gathered_key[0], key_gain, jnp.arange(prefix, dtype=jnp.int32), head_dimension
    )
    rotated_query_rows, query_unit, query_inv, query_cos, query_sin = norm_rope(
        query_raw[0, 0], query_gain, positions, head_dimension
    )
    key_rot, key_unit, key_inv, key_cos, key_sin = norm_rope(
        response_key_input[0, 0], key_gain, positions, head_dimension
    )
    valid_rows = (token_numbers < resp_len[0, 0])[:, None]
    output_gradient = jnp.where(
        valid_rows, grad_out[0, 0].astype(jnp.float32) * advantage, 0.0
    ).astype(jnp.bfloat16)
    joined_keys = jnp.concatenate([pre_rot, key_rot], axis=0).transpose(1, 0, 2)
    value_matrix = jnp.concatenate(
        [
            gathered_value[0].reshape(prefix, kv_heads, head_dimension),
            response_value_input[0, 0].reshape(length, kv_heads, head_dimension),
        ],
        axis=0,
    ).transpose(1, 0, 2)
    query_matrix = (
        rotated_query_rows.reshape(length, kv_heads, responses_per_group, head_dimension)
        .transpose(1, 2, 0, 3)
        .reshape(kv_heads, responses_per_group * length, head_dimension)
    )
    incoming_gradients = (
        output_gradient.reshape(length, kv_heads, responses_per_group, head_dimension)
        .transpose(1, 2, 0, 3)
        .reshape(kv_heads, responses_per_group * length, head_dimension)
    )
    query_gradient_out, dkey_local, dvalue_local, pre_parts = lax.map(
        lambda operands: kv_group(
            operands[0], operands[1], operands[2], operands[3], starting_position, prefix, length
        ),
        (query_matrix, joined_keys, value_matrix, incoming_gradients),
    )
    dquery_rot = (
        query_gradient_out.reshape(kv_heads, responses_per_group, length, head_dimension)
        .transpose(2, 0, 1, 3)
        .reshape(length, query_heads, head_dimension)
    )
    grad_query_rows, query_contribution = norm_rope_back(
        dquery_rot, query_unit, query_inv, query_gain, query_cos, query_sin
    )
    grad_key_rows, key_contribution = norm_rope_back(
        dkey_local.transpose(1, 0, 2), key_unit, key_inv, key_gain, key_cos, key_sin
    )
    grad_value_rows = dvalue_local.transpose(1, 0, 2).reshape(length, kv_cols)
    dkey_pre, prompt_value_gradient = pre_parts
    dkey_pre = dkey_pre.transpose(1, 0, 2)
    prompt_contribution = norm_rope_back(dkey_pre, pre_unit, pre_inv, key_gain, pre_cos, pre_sin)[1]
    gain_terms = jnp.concatenate(
        [split_terms(query_contribution, 2), split_terms(key_contribution + prompt_contribution, 2)]
    )
    gain_rows = jnp.pad(gain_terms, ((0, own_rows - 4), (0, 0)))
    blocks = jnp.concatenate(
        [
            dkey_pre.reshape(responses, own_rows, kv_cols).astype(jnp.bfloat16),
            prompt_value_gradient.transpose(1, 0, 2)
            .reshape(responses, own_rows, kv_cols)
            .astype(jnp.bfloat16),
            jnp.broadcast_to(gain_rows[None], (responses,) + gain_rows.shape),
        ],
        axis=2,
    )
    owned = jnp.sum(lax.all_to_all(blocks, "resp", 0, 0).astype(jnp.float32), axis=0)
    dkey_owned, dvalue_owned = owned[:, :kv_cols], owned[:, kv_cols:kv_width]
    gain_sums = owned[:4, kv_width:]
    gain_sums = jnp.stack([gain_sums[0] + gain_sums[1], gain_sums[2] + gain_sums[3]])
    others = lax.axis_size("dp") * lax.axis_size("tensor")
    totals = jnp.sum(
        lax.all_to_all(
            jnp.broadcast_to(gain_sums[None], (others,) + gain_sums.shape), ("dp", "tensor"), 0, 0
        ),
        axis=0,
    )
    own_positions = lax.axis_index("resp") * own_rows + jnp.arange(own_rows, dtype=jnp.int32)
    owned_rot, owned_unit, owned_inv, owned_cos, owned_sin = norm_rope(
        prompt_key_input[0], key_gain, own_positions, head_dimension
    )
    prompt_key_gradient, _ = norm_rope_back(
        dkey_owned.reshape(own_rows, kv_heads, head_dimension),
        owned_unit,
        owned_inv,
        key_gain,
        owned_cos,
        owned_sin,
    )
    replicas = lax.axis_size("dp") * responses
    return (
        grad_query_rows.reshape(1, 1, length, query_heads * head_dimension).astype(jnp.bfloat16),
        grad_key_rows.reshape(1, 1, length, kv_cols).astype(jnp.bfloat16),
        grad_value_rows.reshape(1, 1, length, kv_cols).astype(jnp.bfloat16),
        prompt_key_gradient.reshape(1, own_rows, kv_cols),
        dvalue_owned.reshape(1, own_rows, kv_cols),
        totals[0] / replicas,
        totals[1] / replicas,
    )


def solution(mesh):
    return jax.shard_map(
        local,
        mesh=mesh,
        in_specs=(
            P("dp", "resp", None, "tensor"),
            P("dp", "resp", None, "tensor"),
            P("dp", "resp", None, "tensor"),
            P("dp", "resp", "tensor"),
            P("dp", "resp", "tensor"),
            P(),
            P(),
            P("dp", "resp", None, "tensor"),
            P("dp", "resp"),
            P("dp", "resp"),
            P("dp"),
        ),
        out_specs=(
            P("dp", "resp", None, "tensor"),
            P("dp", "resp", None, "tensor"),
            P("dp", "resp", None, "tensor"),
            P("dp", "resp", "tensor"),
            P("dp", "resp", "tensor"),
            P(),
            P(),
        ),
        check_vma=False,
    )
```

```python
import functools
import math

import jax
import jax.numpy as jnp
import numpy as np
from jax import lax
from jax.experimental import pallas as pl
from jax.experimental.pallas import tpu as pltpu
from jax.sharding import PartitionSpec as P

EPSILON = 1e-06
THETA = 1000000.0
LOG2_E = math.log2(math.e)
F32, BF16 = jnp.float32, jnp.bfloat16
SMEM = pl.BlockSpec(memory_space=pltpu.SMEM)
VMEM = pl.BlockSpec(memory_space=pltpu.VMEM)
CONTRACT_LAST = (((1,), (1,)), ((), ()))
CONTRACT_FIRST = (((0,), (0,)), ((), ()))
HEADS_AT_ONCE = 2


def rope_tables(positions, width):
    half = width // 2
    inv_freq = (THETA ** (-(np.arange(half) * 2.0) / width)).astype(np.float32)
    angles = (np.arange(positions, dtype=np.float32)[:, None] * inv_freq).astype(np.float64)
    cos, sin = np.cos(angles), np.sin(angles)
    return (
        np.concatenate([cos, cos], axis=1).astype(np.float32),
        np.concatenate([-sin, sin], axis=1).astype(np.float32),
    )


def half_turn(rows):
    return pltpu.roll(rows, rows.shape[1] // 2, 1)


def unit_rows(raw):
    raw = raw.astype(F32)
    inverse = lax.rsqrt(jnp.mean(raw * raw, axis=1, keepdims=True) + EPSILON)
    return raw * inverse, inverse


def rotated(unit, gain, cos, sin):
    normed = unit * gain
    return (normed * cos + half_turn(normed) * sin).astype(BF16)


def norm_rope_back(grad, unit, inverse, gain, cos, sin):
    normed_grad = grad * cos - half_turn(grad) * sin
    term = normed_grad * unit
    mean = jnp.mean(term * gain, axis=1, keepdims=True)
    return inverse * (normed_grad * gain - unit * mean), term


def fold(rows):
    return jnp.sum(rows.reshape(-1, 8, rows.shape[1]), axis=0)


def split_terms(value, terms):
    found = []
    for _ in range(terms):
        found.append(value.astype(BF16).astype(F32))
        value = value - found[-1]
    return found


def send_prompt(reward_ref, key_ref, value_ref, out_ref):
    own, width = key_ref.shape
    lane = lax.broadcasted_iota(jnp.int32, (own, 128), 1)
    reward = jnp.full((own, 128), reward_ref[0, 0], F32)
    first, second, third = split_terms(reward, 3)
    tail = jnp.where(
        lane == 0, first, jnp.where(lane == 1, second, jnp.where(lane == 2, third, 0.0))
    )
    slot = jnp.concatenate([key_ref[...].astype(F32), value_ref[...].astype(F32), tail], axis=1)
    slots = jnp.concatenate([slot, slot], axis=0).astype(BF16)
    for i in range(out_ref.shape[0] // (2 * own)):
        out_ref[2 * own * i : 2 * own * (i + 1), :] = slots


def prepare(prompt_len_ref, query_ref, key_ref, query_gain_ref, key_gain_ref, cos_ref, sin_ref,
            query_out, key_out):
    length, width = query_ref.shape[0], query_gain_ref.shape[1]
    start = prompt_len_ref[0]
    cos, sin = cos_ref[pl.ds(start, length), :], sin_ref[pl.ds(start, length), :]
    for source, gain_ref, out in (
        (key_ref, key_gain_ref, key_out),
        (query_ref, query_gain_ref, query_out),
    ):
        gain = gain_ref[...]

        def one(h, _, source=source, gain=gain, out=out):
            raw = source[:, pl.ds(pl.multiple_of(h * width, width), width)]
            rows = rotated(unit_rows(raw)[0], gain, cos, sin)
            out[pl.ds(pl.multiple_of(h * length, length), length), :] = rows
            return 0

        heads = source.shape[1] // width
        lax.fori_loop(0, heads, one, 0, unroll=2)


def attend(
    reward_ref, resp_len_ref, prompt_len_ref,
    arrived_ref, query_ref, key_ref, raw_query_ref, raw_key_ref, value_ref, grad_ref,
    query_gain_ref, key_gain_ref, cos_ref, sin_ref,
    query_out, key_out, value_out, blocks_out,
    keys, values, key_sum, value_sum, query_terms, key_terms, *, responses,
):
    length, width = grad_ref.shape[0], query_gain_ref.shape[1]
    prefix = arrived_ref.shape[0]
    kv_heads = raw_key_ref.shape[1] // width
    kv_cols = kv_heads * width
    group = grad_ref.shape[1] // kv_cols
    own = prefix // responses
    scale = width**-0.5
    start = prompt_len_ref[0]
    query_gain, key_gain = query_gain_ref[...], key_gain_ref[...]
    cos, sin = cos_ref[pl.ds(start, length), :], sin_ref[pl.ds(start, length), :]
    pre_cos, pre_sin = cos_ref[:prefix, :], sin_ref[:prefix, :]

    reward_sum = jnp.sum(arrived_ref[:, 2 * kv_cols :].astype(F32)) / own
    advantage = reward_ref[0, 0] - reward_sum / responses
    token = lax.broadcasted_iota(jnp.int32, (length, width), 0)
    factor = jnp.where(token < resp_len_ref[0, 0], advantage, 0.0)
    query_terms[...] = jnp.zeros_like(query_terms)
    key_terms[...] = jnp.zeros_like(key_terms)

    def one_kv_head(c, _):
        own_cols = pl.ds(pl.multiple_of(c * width, width), width)
        value_cols = pl.ds(pl.multiple_of(kv_cols + c * width, width), width)
        pre_unit, pre_inverse = unit_rows(arrived_ref[:, own_cols])
        keys[:prefix, :] = rotated(pre_unit, key_gain, pre_cos, pre_sin)
        keys[prefix:, :] = key_ref[pl.ds(pl.multiple_of(c * length, length), length), :]
        values[:prefix, :] = arrived_ref[:, value_cols]
        values[prefix:, :] = value_ref[:, own_cols]
        key_sum[...] = jnp.zeros_like(key_sum)
        value_sum[...] = jnp.zeros_like(value_sum)

        def some_heads(p, _):
            first = c * group + p * HEADS_AT_ONCE
            count = HEADS_AT_ONCE * length
            query_rows = query_ref[pl.ds(pl.multiple_of(first * length, length), count), :]
            heads = [
                pl.ds(pl.multiple_of((first + i) * width, width), width)
                for i in range(HEADS_AT_ONCE)
            ]
            grad_rows = jnp.concatenate(
                [(grad_ref[:, cols].astype(F32) * factor).astype(BF16) for cols in heads], axis=0
            )
            score = lax.dot_general(
                keys[...], query_rows, CONTRACT_LAST, preferred_element_type=F32
            )
            expo = jnp.exp2(score * (scale * LOG2_E))
            row = lax.broadcasted_iota(jnp.int32, (prefix, count), 0)
            resp_row = lax.broadcasted_iota(jnp.int32, (length, count), 0)
            query_token = lax.broadcasted_iota(jnp.int32, (length, count), 1) % length
            expo = jnp.concatenate(
                [
                    jnp.where(row < start, expo[:prefix], 0.0),
                    jnp.where(resp_row <= query_token, expo[prefix:], 0.0),
                ],
                axis=0,
            )
            prob = expo * (1.0 / jnp.sum(expo, axis=0, keepdims=True))
            dprob = lax.dot_general(
                values[...], grad_rows, CONTRACT_LAST, preferred_element_type=F32
            )
            delta = jnp.sum(prob * dprob, axis=0, keepdims=True)
            dscore = (prob * (dprob - delta) * scale).astype(BF16)
            key_sum[...] += jnp.dot(dscore, query_rows, preferred_element_type=F32)
            value_sum[...] += jnp.dot(prob.astype(BF16), grad_rows, preferred_element_type=F32)
            query_grad = lax.dot_general(
                dscore, keys[...], CONTRACT_FIRST, preferred_element_type=F32
            )
            for i, cols in enumerate(heads):
                unit, inverse = unit_rows(raw_query_ref[:, cols])
                raw_grad, term = norm_rope_back(
                    query_grad[i * length : (i + 1) * length], unit, inverse, query_gain, cos, sin
                )
                query_out[:, cols] = raw_grad.astype(BF16)
                query_terms[...] += fold(term)
            return 0

        lax.fori_loop(0, group // HEADS_AT_ONCE, some_heads, 0)
        raw_grad, term = norm_rope_back(
            key_sum[:prefix, :], pre_unit, pre_inverse, key_gain, pre_cos, pre_sin
        )
        blocks_out[:, own_cols] = raw_grad.astype(BF16)
        blocks_out[:, value_cols] = value_sum[:prefix, :].astype(BF16)
        key_terms[...] += fold(term)
        unit, inverse = unit_rows(raw_key_ref[:, own_cols])
        raw_grad, term = norm_rope_back(key_sum[prefix:, :], unit, inverse, key_gain, cos, sin)
        key_out[:, own_cols] = raw_grad.astype(BF16)
        value_out[:, own_cols] = value_sum[prefix:, :].astype(BF16)
        key_terms[...] += fold(term)
        return 0

    lax.fori_loop(0, kv_heads, one_kv_head, 0)
    slot_row = lax.broadcasted_iota(jnp.int32, (own, width), 0)
    gains = jnp.zeros((own, width), F32)
    for i, terms in enumerate((query_terms, key_terms)):
        high, low = split_terms(jnp.sum(terms[...], axis=0, keepdims=True), 2)
        gains = jnp.where(slot_row == 2 * i, high, jnp.where(slot_row == 2 * i + 1, low, gains))
    pair = jnp.concatenate([gains, gains], axis=0).astype(BF16)
    for i in range(responses // 2):
        blocks_out[2 * own * i : 2 * own * (i + 1), 2 * kv_cols :] = pair


def add_blocks(arrived_ref, key_out, value_out, gains_out):
    kv_cols = key_out.shape[1]
    own = key_out.shape[0]
    total = jnp.zeros((2 * own, arrived_ref.shape[1]), F32)
    for i in range(arrived_ref.shape[0] // (2 * own)):
        total += arrived_ref[2 * own * i : 2 * own * (i + 1), :].astype(F32)
    total = total[:own] + total[own:]
    key_out[...] = total[:, :kv_cols]
    value_out[...] = total[:, kv_cols : 2 * kv_cols]
    gains = total[:, 2 * kv_cols :]
    row = lax.broadcasted_iota(jnp.int32, gains.shape, 0)
    query = jnp.sum(jnp.where(row < 2, gains, 0.0), axis=0, keepdims=True)
    key = jnp.sum(jnp.where(row < 2, 0.0, gains), axis=0, keepdims=True)
    row = lax.broadcasted_iota(jnp.int32, gains_out.shape, 0)
    gains_out[...] = jnp.where(row % 2 == 0, query, key)


def local(
    query_raw, response_key_input, response_value_input, prompt_key_input, prompt_value_input,
    query_gain, key_gain, grad_out, rewards, resp_len, prompt_len,
):
    length = query_raw.shape[2]
    width = query_gain.shape[0]
    kv_cols = response_key_input.shape[3]
    kv_heads = kv_cols // width
    query_heads = query_raw.shape[3] // width
    responses = lax.axis_size("resp")
    own = prompt_key_input.shape[1]
    prefix = own * responses
    slot_cols = 2 * kv_cols + width
    cos, sin = (jnp.asarray(t) for t in rope_tables(prefix + length, width))
    gains = (query_gain.reshape(1, width), key_gain.reshape(1, width))
    query, key = query_raw[0, 0], response_key_input[0, 0]
    shape = jax.ShapeDtypeStruct

    slots = pl.pallas_call(
        send_prompt,
        out_shape=shape((prefix, slot_cols), BF16),
        in_specs=[SMEM, VMEM, VMEM],
        out_specs=VMEM,
        name="send_prompt",
    )(rewards, prompt_key_input[0], prompt_value_input[0])
    arrived = lax.all_to_all(slots.reshape(responses, own, slot_cols), "resp", 0, 0)
    rotated_query, rotated_key = pl.pallas_call(
        prepare,
        out_shape=(shape((query_heads * length, width), BF16), shape((kv_heads * length, width), BF16)),
        in_specs=[SMEM] + [VMEM] * 6,
        out_specs=(VMEM, VMEM),
        name="prepare",
        cost_estimate=pl.CostEstimate(flops=20_000_000, bytes_accessed=2_000_000, transcendentals=0),
    )(prompt_len, query, key, *gains, cos, sin)
    grad_query, grad_key, grad_value, blocks = pl.pallas_call(
        functools.partial(attend, responses=responses),
        out_shape=(
            shape(query.shape, BF16),
            shape(key.shape, BF16),
            shape(key.shape, BF16),
            shape((prefix, slot_cols), BF16),
        ),
        in_specs=[SMEM] * 3 + [VMEM] * 11,
        out_specs=(VMEM,) * 4,
        scratch_shapes=[
            pltpu.VMEM((prefix + length, width), BF16),
            pltpu.VMEM((prefix + length, width), BF16),
            pltpu.VMEM((prefix + length, width), F32),
            pltpu.VMEM((prefix + length, width), F32),
            pltpu.VMEM((8, width), F32),
            pltpu.VMEM((8, width), F32),
        ],
        compiler_params=pltpu.CompilerParams(vmem_limit_bytes=32 * 2**20),
        name="attend",
    )(
        rewards, resp_len, prompt_len,
        arrived.reshape(prefix, slot_cols), rotated_query, rotated_key, query, key,
        response_value_input[0, 0], grad_out[0, 0], *gains, cos, sin,
    )
    summed = lax.all_to_all(blocks.reshape(responses, own, slot_cols), "resp", 0, 0)
    others = lax.axis_size("dp") * lax.axis_size("tensor")
    prefix_key, prefix_value, gain_slots = pl.pallas_call(
        add_blocks,
        out_shape=(
            shape((own, kv_cols), F32),
            shape((own, kv_cols), F32),
            shape((others * 2, width), F32),
        ),
        in_specs=[VMEM],
        out_specs=(VMEM,) * 3,
        name="add_blocks",
    )(summed.reshape(prefix, slot_cols))
    gain_slots = lax.all_to_all(
        gain_slots.reshape(others, 2, width), ("dp", "tensor"), 0, 0
    )
    totals = jnp.sum(gain_slots, axis=0) / (lax.axis_size("dp") * responses)
    return (
        grad_query[None, None],
        grad_key[None, None],
        grad_value[None, None],
        prefix_key[None],
        prefix_value[None],
        totals[0],
        totals[1],
    )


def solution(mesh):
    token_spec = P("dp", "resp", None, "tensor")
    prompt_spec = P("dp", "resp", "tensor")
    return jax.shard_map(
        local,
        mesh=mesh,
        in_specs=(token_spec,) * 3 + (prompt_spec,) * 2 + (P(), P(), token_spec)
        + (P("dp", "resp"), P("dp", "resp"), P("dp")),
        out_specs=(token_spec,) * 3 + (prompt_spec,) * 2 + (P(), P()),
        check_vma=False,
    )
```

```python
import functools
import math

import jax
import jax.numpy as jnp
import numpy as np
from jax import lax
from jax.experimental import pallas as pl
from jax.experimental.pallas import tpu as pltpu
from jax.sharding import PartitionSpec as P

EPSILON = 1e-06
THETA = 1000000.0
LOG2_E = math.log2(math.e)
F32, BF16 = jnp.float32, jnp.bfloat16
SMEM = pl.BlockSpec(memory_space=pltpu.SMEM)
VMEM = pl.BlockSpec(memory_space=pltpu.VMEM)
CONTRACT_LAST = (((1,), (1,)), ((), ()))
CONTRACT_FIRST = (((0,), (0,)), ((), ()))
HEADS_AT_ONCE = 4
STEP = 16
UNROLL = 1
UNROLL_KV = 1


def rope_tables(positions, width):
    half = width // 2
    inv_freq = (THETA ** (-(np.arange(half) * 2.0) / width)).astype(np.float32)
    rows = [np.arange(STEP), np.arange(0, positions, STEP)]
    angles = [r[:, None].astype(np.float64) * inv_freq for r in rows]
    sign = np.repeat([-1.0, 1.0], half)
    found = []
    for angle in angles:
        angle = np.concatenate([angle, angle], axis=1)
        found += [np.cos(angle), np.sin(angle) * sign]
    return np.concatenate(found, axis=0).astype(np.float32)


def add_angles(one, other):
    return one[0] * other[0] - one[1] * other[1], one[1] * other[0] + one[0] * other[1]


def rope_at(table_ref, start, count):
    steps = (table_ref.shape[0] - 2 * STEP) // 2
    low = (table_ref[:STEP, :], table_ref[STEP : 2 * STEP, :])

    def high(m):
        first = 2 * STEP + m
        return table_ref[pl.ds(first, 1), :], table_ref[pl.ds(first + steps, 1), :]

    if not isinstance(start, int):
        within = start % STEP
        row = (table_ref[pl.ds(within, 1), :], table_ref[pl.ds(STEP + within, 1), :])
        low = add_angles(low, add_angles(high(start // STEP), row))
    blocks = [add_angles(low, high(m)) for m in range(count // STEP)]
    return tuple(jnp.concatenate([block[i] for block in blocks], axis=0) for i in range(2))


def half_turn(rows):
    return pltpu.roll(rows, rows.shape[1] // 2, 1)


def unit_rows(raw):
    raw = raw.astype(F32)
    inverse = lax.rsqrt(jnp.mean(raw * raw, axis=1, keepdims=True) + EPSILON)
    return raw * inverse, inverse


def rotated(unit, gain, cos, sin):
    normed = unit * gain
    return (normed * cos + half_turn(normed) * sin).astype(BF16)


def norm_rope_back(grad, unit, inverse, gain, cos, sin):
    normed_grad = grad * cos - half_turn(grad) * sin
    term = normed_grad * unit
    mean = jnp.mean(term * gain, axis=1, keepdims=True)
    return inverse * (normed_grad * gain - unit * mean), term


def fold(rows):
    return jnp.sum(rows.reshape(-1, 8, rows.shape[1]), axis=0)


def split_terms(value, terms):
    found = []
    for _ in range(terms):
        found.append(value.astype(BF16).astype(F32))
        value = value - found[-1]
    return found


def send_prompt(key_ref, value_ref, out_ref):
    own = key_ref.shape[0]
    slot = jnp.concatenate([key_ref[...], value_ref[...]], axis=1).astype(F32)
    slots = jnp.concatenate([slot, slot], axis=0).astype(BF16)
    for i in range(out_ref.shape[0] // (2 * own)):
        out_ref[2 * own * i : 2 * own * (i + 1), :] = slots


def head_slices(first, width):
    return [
        pl.ds(pl.multiple_of((first + i) * width, width), width) for i in range(HEADS_AT_ONCE)
    ]


def prepare(
    prompt_len_ref, query_ref, key_ref, query_gain_ref, key_gain_ref, table_ref,
    query_out, key_out, shared_out,
):
    length, width = query_ref.shape[0], query_gain_ref.shape[1]
    cos, sin = rope_at(table_ref, prompt_len_ref[0], length)
    shared_out[: table_ref.shape[0], :] = table_ref[...]
    shared_out[table_ref.shape[0] :, :] = jnp.concatenate(
        [query_gain_ref[...], key_gain_ref[...], jnp.zeros((6, width), F32)], axis=0
    )
    for source, gain_ref, out in (
        (key_ref, key_gain_ref, key_out),
        (query_ref, query_gain_ref, query_out),
    ):
        gain = gain_ref[...]

        def one(h, _, source=source, gain=gain, out=out):
            raw = source[:, pl.ds(pl.multiple_of(h * width, width), width)]
            rows = rotated(unit_rows(raw)[0], gain, cos, sin)
            out[pl.ds(pl.multiple_of(h * length, length), length), :] = rows
            return 0

        lax.fori_loop(0, source.shape[1] // width, one, 0, unroll=2)


def attend(
    reward_ref, resp_len_ref, prompt_len_ref,
    arrived_ref, query_ref, key_ref, shared_ref, raw_query_ref, raw_key_ref, value_ref, grad_ref,
    query_hbm, key_hbm, value_hbm, blocks_out,
    keys, values, key_sum, value_sum, query_terms, key_terms, query_out, key_out, value_out, sems,
    *, responses,
):
    length, width = grad_ref.shape[0], shared_ref.shape[1]
    prefix = arrived_ref.shape[0]
    kv_heads = raw_key_ref.shape[1] // width
    kv_cols = kv_heads * width
    group = grad_ref.shape[1] // kv_cols
    own = prefix // responses
    count = HEADS_AT_ONCE * length
    scale = width**-0.5
    start = prompt_len_ref[0]
    table_ref = shared_ref.at[: shared_ref.shape[0] - 8]
    query_gain, key_gain = (shared_ref[pl.ds(shared_ref.shape[0] - 8 + i, 1), :] for i in range(2))
    cos, sin = rope_at(table_ref, start, length)
    pre_cos, pre_sin = rope_at(table_ref, 0, prefix)

    valid = lax.broadcasted_iota(jnp.int32, (1, count), 1) % length < resp_len_ref[0, 0]
    visible = lax.broadcasted_iota(jnp.int32, (prefix, count), 0) < start
    causal = lax.broadcasted_iota(jnp.int32, (length, count), 0) <= (
        lax.broadcasted_iota(jnp.int32, (length, count), 1) % length
    )
    query_terms[...] = jnp.zeros_like(query_terms)
    key_terms[...] = jnp.zeros_like(key_terms)

    def query_copy(first):
        cols = pl.ds(pl.multiple_of(first * width, width), HEADS_AT_ONCE * width)
        return pltpu.make_async_copy(
            query_out.at[:, cols], query_hbm.at[:, cols], sems.at[first // HEADS_AT_ONCE]
        )

    def one_kv_head(c, _):
        own_cols = pl.ds(pl.multiple_of(c * width, width), width)
        value_cols = pl.ds(pl.multiple_of(kv_cols + c * width, width), width)
        pre_unit, pre_inverse = unit_rows(arrived_ref[:, own_cols])
        keys[:prefix, :] = rotated(pre_unit, key_gain, pre_cos, pre_sin)
        keys[prefix:, :] = key_ref[pl.ds(pl.multiple_of(c * length, length), length), :]
        values[:prefix, :] = arrived_ref[:, value_cols]
        values[prefix:, :] = value_ref[:, own_cols]
        key_sum[...] = jnp.zeros_like(key_sum)
        value_sum[...] = jnp.zeros_like(value_sum)

        def some_heads(p, _):
            first = c * group + p * HEADS_AT_ONCE
            span = pl.ds(pl.multiple_of(first * length, count), count)
            query_rows = query_ref[span, :]
            heads = head_slices(first, width)
            grad_rows = jnp.concatenate([grad_ref[:, cols] for cols in heads], axis=0)
            score = lax.dot_general(
                keys[...], query_rows, CONTRACT_LAST, preferred_element_type=F32
            )
            expo = jnp.exp2(score * (scale * LOG2_E))
            expo = jnp.concatenate(
                [
                    jnp.where(visible, expo[:prefix], 0.0),
                    jnp.where(causal, expo[prefix:], 0.0),
                ],
                axis=0,
            )
            dprob = lax.dot_general(
                values[...], grad_rows, CONTRACT_LAST, preferred_element_type=F32
            )
            inverse_sum = 1.0 / jnp.sum(expo, axis=0, keepdims=True)
            delta = jnp.sum(expo * dprob, axis=0, keepdims=True) * inverse_sum
            weight = jnp.where(valid, inverse_sum, 0.0)
            dscore = (expo * ((dprob - delta) * (weight * scale))).astype(BF16)
            prob = (expo * weight).astype(BF16)
            key_sum[...] += jnp.dot(dscore, query_rows, preferred_element_type=F32)
            value_sum[...] += jnp.dot(prob, grad_rows, preferred_element_type=F32)
            query_grad = lax.dot_general(
                dscore, keys[...], CONTRACT_FIRST, preferred_element_type=F32
            )
            for i, cols in enumerate(heads):
                unit, inverse = unit_rows(raw_query_ref[:, cols])
                raw_grad, term = norm_rope_back(
                    query_grad[i * length : (i + 1) * length], unit, inverse, query_gain, cos, sin
                )
                query_out[:, cols] = raw_grad
                query_terms[...] += fold(term)
            query_copy(first).start()
            return 0

        lax.fori_loop(0, group // HEADS_AT_ONCE, some_heads, 0, unroll=UNROLL)
        raw_grad, term = norm_rope_back(
            key_sum[:prefix, :], pre_unit, pre_inverse, key_gain, pre_cos, pre_sin
        )
        blocks_out[:, own_cols] = raw_grad.astype(BF16)
        blocks_out[:, value_cols] = value_sum[:prefix, :].astype(BF16)
        key_terms[...] += fold(term)
        unit, inverse = unit_rows(raw_key_ref[:, own_cols])
        raw_grad, term = norm_rope_back(key_sum[prefix:, :], unit, inverse, key_gain, cos, sin)
        key_out[:, own_cols] = raw_grad
        value_out[:, own_cols] = value_sum[prefix:, :]
        key_terms[...] += fold(term)
        return 0

    lax.fori_loop(0, kv_heads, one_kv_head, 0, unroll=UNROLL_KV)
    last_copies = [
        pltpu.make_async_copy(key_out, key_hbm, sems.at[kv_heads * group // HEADS_AT_ONCE]),
        pltpu.make_async_copy(value_out, value_hbm, sems.at[kv_heads * group // HEADS_AT_ONCE + 1]),
    ]
    for copy in last_copies:
        copy.start()
    reward = jnp.full((1, width), reward_ref[0, 0], F32)
    rows = split_terms(jnp.sum(query_terms[...], axis=0, keepdims=True), 2)
    rows += split_terms(jnp.sum(key_terms[...], axis=0, keepdims=True), 2)
    rows += split_terms(reward, 3)
    rows = jnp.concatenate(rows + [jnp.zeros((own - len(rows), width), F32)], axis=0)
    pair = jnp.concatenate([rows, rows], axis=0).astype(BF16)
    for i in range(responses // 2):
        blocks_out[2 * own * i : 2 * own * (i + 1), 2 * kv_cols :] = pair
    for copy in [query_copy(h) for h in range(0, kv_heads * group, HEADS_AT_ONCE)] + last_copies:
        copy.wait()


def advantages(tail, responses):
    tail = tail.astype(F32).reshape(responses, -1, tail.shape[1])
    row = lax.broadcasted_iota(jnp.int32, tail.shape, 1)
    reward = jnp.sum(jnp.where((row >= 4) & (row < 7), tail, 0.0), axis=1, keepdims=True)
    mean = jnp.sum(reward, axis=0, keepdims=True) / responses
    return tail, jnp.broadcast_to(reward - mean, tail.shape), mean[0]


def weigh(blocks_ref, gains_out, *, responses):
    width = gains_out.shape[1]
    tail, weights, _ = advantages(blocks_ref[:, blocks_ref.shape[1] - width :], responses)
    terms = jnp.sum(tail * weights, axis=0)
    query, key = terms[0:1] + terms[1:2], terms[2:3] + terms[3:4]
    row = lax.broadcasted_iota(jnp.int32, gains_out.shape, 0)
    gains_out[...] = jnp.where(row % 2 == 0, query, key)


def finish(
    reward_ref, blocks_ref, query_ref, key_ref, value_ref,
    query_out, key_out, value_out, prefix_key_out, prefix_value_out, *, responses,
):
    own, kv_cols = prefix_key_out.shape
    width = blocks_ref.shape[1] - 2 * kv_cols
    _, weights, mean = advantages(blocks_ref[:, 2 * kv_cols :], responses)
    for out, first in ((prefix_key_out, 0), (prefix_value_out, kv_cols)):
        for cols in range(0, kv_cols, width):
            block = blocks_ref[:, first + cols : first + cols + width].astype(F32)
            out[:, cols : cols + width] = jnp.sum(block.reshape(weights.shape) * weights, axis=0)
    weight = (reward_ref[0, 0] - mean)[:, :1]
    for source, out in ((query_ref, query_out), (key_ref, key_out), (value_ref, value_out)):
        out[...] = (source[...] * weight).astype(BF16)


def local(
    query_raw, response_key_input, response_value_input, prompt_key_input, prompt_value_input,
    query_gain, key_gain, grad_out, rewards, resp_len, prompt_len,
):
    length = query_raw.shape[2]
    width = query_gain.shape[0]
    kv_cols = response_key_input.shape[3]
    kv_heads = kv_cols // width
    query_heads = query_raw.shape[3] // width
    responses = lax.axis_size("resp")
    own = prompt_key_input.shape[1]
    prefix = own * responses
    slot_cols = 2 * kv_cols + width
    table = jnp.asarray(rope_tables(prefix + length, width))
    gains = (query_gain.reshape(1, width), key_gain.reshape(1, width))
    query, key, value, grad = (
        a[0, 0] for a in (query_raw, response_key_input, response_value_input, grad_out)
    )
    shape = jax.ShapeDtypeStruct

    slots = pl.pallas_call(
        send_prompt,
        out_shape=pltpu.VMEM((prefix, 2 * kv_cols), BF16),
        in_specs=[VMEM] * 2,
        out_specs=VMEM,
        name="send_prompt",
    )(prompt_key_input[0], prompt_value_input[0])
    arrived = lax.all_to_all(slots.reshape(responses, own, 2 * kv_cols), "resp", 0, 0)
    prepared = pl.pallas_call(
        prepare,
        out_shape=(
            pltpu.VMEM((query_heads * length, width), BF16),
            pltpu.VMEM((kv_heads * length, width), BF16),
            pltpu.VMEM((table.shape[0] + 8, width), F32),
        ),
        in_specs=[SMEM] + [VMEM] * 5,
        out_specs=(VMEM,) * 3,
        cost_estimate=pl.CostEstimate(
            flops=100_000_000, bytes_accessed=4_000_000, transcendentals=0
        ),
        name="prepare",
    )(prompt_len, query, key, *gains, table)
    *grads, blocks = pl.pallas_call(
        functools.partial(attend, responses=responses),
        out_shape=(
            pltpu.HBM(query.shape, F32),
            pltpu.HBM(key.shape, F32),
            pltpu.HBM(key.shape, F32),
            pltpu.VMEM((prefix, slot_cols), BF16),
        ),
        in_specs=[SMEM] * 3 + [VMEM] * 8,
        out_specs=(pl.BlockSpec(memory_space=pltpu.HBM),) * 3 + (VMEM,),
        scratch_shapes=[
            pltpu.VMEM((prefix + length, width), BF16),
            pltpu.VMEM((prefix + length, width), BF16),
            pltpu.VMEM((prefix + length, width), F32),
            pltpu.VMEM((prefix + length, width), F32),
            pltpu.VMEM((8, width), F32),
            pltpu.VMEM((8, width), F32),
            pltpu.VMEM(query.shape, F32),
            pltpu.VMEM(key.shape, F32),
            pltpu.VMEM(key.shape, F32),
            pltpu.SemaphoreType.DMA((query_heads // HEADS_AT_ONCE + 2,)),
        ],
        compiler_params=pltpu.CompilerParams(vmem_limit_bytes=16 * 2**20),
        name="attend",
    )(
        rewards, resp_len, prompt_len, arrived.reshape(prefix, 2 * kv_cols), *prepared,
        query, key, value, grad,
    )
    received = lax.all_to_all(blocks.reshape(responses, own, slot_cols), "resp", 0, 0)
    received = pltpu.with_memory_space_constraint(
        received.reshape(prefix, slot_cols), pltpu.VMEM
    )
    others = lax.axis_size("dp") * lax.axis_size("tensor")
    gain_slots = pl.pallas_call(
        functools.partial(weigh, responses=responses),
        out_shape=pltpu.VMEM((others * 2, width), F32),
        in_specs=[VMEM],
        out_specs=VMEM,
        name="weigh",
    )(received)
    gain_slots = lax.all_to_all(gain_slots.reshape(others, 2, width), ("dp", "tensor"), 0, 0)
    grad_query, grad_key, grad_value, prefix_key, prefix_value = pl.pallas_call(
        functools.partial(finish, responses=responses),
        out_shape=(
            shape(query.shape, BF16),
            shape(key.shape, BF16),
            shape(key.shape, BF16),
            shape((own, kv_cols), F32),
            shape((own, kv_cols), F32),
        ),
        in_specs=[SMEM] + [VMEM] * 4,
        out_specs=(VMEM,) * 5,
        cost_estimate=pl.CostEstimate(
            flops=10_000_000, bytes_accessed=4_000_000, transcendentals=0
        ),
        name="finish",
    )(rewards, received, *grads)
    totals = jnp.sum(gain_slots, axis=0) / (lax.axis_size("dp") * responses)
    return (
        grad_query[None, None],
        grad_key[None, None],
        grad_value[None, None],
        prefix_key[None],
        prefix_value[None],
        totals[0],
        totals[1],
    )


def solution(mesh):
    token_spec = P("dp", "resp", None, "tensor")
    prompt_spec = P("dp", "resp", "tensor")
    return jax.shard_map(
        local,
        mesh=mesh,
        in_specs=(token_spec,) * 3 + (prompt_spec,) * 2 + (P(), P(), token_spec)
        + (P("dp", "resp"), P("dp", "resp"), P("dp")),
        out_specs=(token_spec,) * 3 + (prompt_spec,) * 2 + (P(), P()),
        check_vma=False,
    )
```

```python
import functools
import math

import jax
import jax.numpy as jnp
import numpy as np
from jax import lax
from jax.experimental import pallas as pl
from jax.experimental.pallas import tpu as pltpu
from jax.sharding import PartitionSpec as P

EPSILON = 1e-06
THETA = 1000000.0
LOG2_E = math.log2(math.e)
F32, BF16 = jnp.float32, jnp.bfloat16
SMEM = pl.BlockSpec(memory_space=pltpu.SMEM)
VMEM = pl.BlockSpec(memory_space=pltpu.VMEM)
CONTRACT_LAST = (((1,), (1,)), ((), ()))
CONTRACT_FIRST = (((0,), (0,)), ((), ()))
HEADS_AT_ONCE = 2
STEP = 16
UNROLL = 2


def rope_tables(positions, width):
    half = width // 2
    inv_freq = (THETA ** (-(np.arange(half) * 2.0) / width)).astype(np.float32)
    rows = [np.arange(STEP), np.arange(0, positions, STEP)]
    angles = [r[:, None].astype(np.float64) * inv_freq for r in rows]
    sign = np.repeat([-1.0, 1.0], half)
    found = []
    for angle in angles:
        angle = np.concatenate([angle, angle], axis=1)
        found += [np.cos(angle), np.sin(angle) * sign]
    return np.concatenate(found, axis=0).astype(np.float32)


def add_angles(one, other):
    return one[0] * other[0] - one[1] * other[1], one[1] * other[0] + one[0] * other[1]


def rope_at(table_ref, start, count):
    steps = (table_ref.shape[0] - 2 * STEP) // 2
    low = (table_ref[:STEP, :], table_ref[STEP : 2 * STEP, :])

    def high(m):
        first = 2 * STEP + m
        return table_ref[pl.ds(first, 1), :], table_ref[pl.ds(first + steps, 1), :]

    if not isinstance(start, int):
        within = start % STEP
        row = (table_ref[pl.ds(within, 1), :], table_ref[pl.ds(STEP + within, 1), :])
        low = add_angles(low, add_angles(high(start // STEP), row))
    blocks = [add_angles(low, high(m)) for m in range(count // STEP)]
    return tuple(jnp.concatenate([block[i] for block in blocks], axis=0) for i in range(2))


def half_turn(rows):
    return pltpu.roll(rows, rows.shape[1] // 2, 1)


def unit_rows(raw):
    raw = raw.astype(F32)
    inverse = lax.rsqrt(jnp.mean(raw * raw, axis=1, keepdims=True) + EPSILON)
    return raw * inverse, inverse


def rotated(unit, gain, cos, sin):
    normed = unit * gain
    return (normed * cos + half_turn(normed) * sin).astype(BF16)


def norm_rope_back(grad, unit, inverse, gain, cos, sin):
    normed_grad = grad * cos - half_turn(grad) * sin
    term = normed_grad * unit
    mean = jnp.mean(term * gain, axis=1, keepdims=True)
    return inverse * (normed_grad * gain - unit * mean), term


def fold(rows):
    return jnp.sum(rows.reshape(-1, 8, rows.shape[1]), axis=0)


def split_terms(value, terms):
    found = []
    for _ in range(terms):
        found.append(value.astype(BF16).astype(F32))
        value = value - found[-1]
    return found


def send_prompt(key_ref, value_ref, out_ref):
    own = key_ref.shape[0]
    slot = jnp.concatenate([key_ref[...], value_ref[...]], axis=1).astype(F32)
    slots = jnp.concatenate([slot, slot], axis=0).astype(BF16)
    for i in range(out_ref.shape[0] // (2 * own)):
        out_ref[2 * own * i : 2 * own * (i + 1), :] = slots


def head_slices(first, width):
    return [
        pl.ds(pl.multiple_of((first + i) * width, width), width) for i in range(HEADS_AT_ONCE)
    ]


def prepare(
    prompt_len_ref, query_ref, key_ref, query_gain_ref, key_gain_ref, table_ref,
    query_out, key_out, shared_out,
):
    length, width = query_ref.shape[0], query_gain_ref.shape[1]
    cos, sin = rope_at(table_ref, prompt_len_ref[0], length)
    shared_out[: table_ref.shape[0], :] = table_ref[...]
    shared_out[table_ref.shape[0] :, :] = jnp.concatenate(
        [query_gain_ref[...], key_gain_ref[...], jnp.zeros((6, width), F32)], axis=0
    )
    for source, gain_ref, out in (
        (key_ref, key_gain_ref, key_out),
        (query_ref, query_gain_ref, query_out),
    ):
        gain = gain_ref[...]

        def one(h, _, source=source, gain=gain, out=out):
            raw = source[:, pl.ds(pl.multiple_of(h * width, width), width)]
            rows = rotated(unit_rows(raw)[0], gain, cos, sin)
            out[pl.ds(pl.multiple_of(h * length, length), length), :] = rows
            return 0

        lax.fori_loop(0, source.shape[1] // width, one, 0, unroll=2)


def attend(
    reward_ref, resp_len_ref, prompt_len_ref,
    arrived_ref, query_ref, key_ref, shared_ref, raw_query_ref, raw_key_ref, value_ref, grad_ref,
    query_hbm, key_hbm, value_hbm, blocks_out,
    keys, values, key_sum, value_sum, query_terms, key_terms, query_out, key_out, value_out, sems,
    *, responses,
):
    length, width = grad_ref.shape[0], shared_ref.shape[1]
    prefix = arrived_ref.shape[0]
    kv_heads = raw_key_ref.shape[1] // width
    kv_cols = kv_heads * width
    group = grad_ref.shape[1] // kv_cols
    own = prefix // responses
    count = HEADS_AT_ONCE * length
    scale = width**-0.5
    start = prompt_len_ref[0]
    table_ref = shared_ref.at[: shared_ref.shape[0] - 8]
    query_gain, key_gain = (shared_ref[pl.ds(shared_ref.shape[0] - 8 + i, 1), :] for i in range(2))
    back_cos, back_sin = (t * scale for t in rope_at(table_ref, start, length))
    pre_cos, pre_sin = rope_at(table_ref, 0, prefix)

    valid = lax.broadcasted_iota(jnp.int32, (1, count), 1) % length < resp_len_ref[0, 0]
    visible = lax.broadcasted_iota(jnp.int32, (prefix, count), 0) < start
    causal = lax.broadcasted_iota(jnp.int32, (length, count), 0) <= (
        lax.broadcasted_iota(jnp.int32, (length, count), 1) % length
    )
    query_terms[...] = jnp.zeros_like(query_terms)
    key_terms[...] = jnp.zeros_like(key_terms)

    def query_copy(first):
        cols = pl.ds(pl.multiple_of(first * width, width), HEADS_AT_ONCE * width)
        return pltpu.make_async_copy(
            query_out.at[:, cols], query_hbm.at[:, cols], sems.at[first // HEADS_AT_ONCE]
        )

    units = []
    for c in range(kv_heads):
        unit = unit_rows(arrived_ref[:, c * width : (c + 1) * width])
        units.append(unit)
        keys[c, :prefix, :] = rotated(unit[0], key_gain, pre_cos, pre_sin)
        keys[c, prefix:, :] = key_ref[c * length : (c + 1) * length, :]
        values[c, :prefix, :] = arrived_ref[:, kv_cols + c * width : kv_cols + (c + 1) * width]
        values[c, prefix:, :] = value_ref[:, c * width : (c + 1) * width]
    key_sum[...] = jnp.zeros_like(key_sum)
    value_sum[...] = jnp.zeros_like(value_sum)

    def products(c, first):
        span = pl.ds(pl.multiple_of(first * length, length), count)
        query_rows = query_ref[span, :]
        grad_rows = jnp.concatenate(
            [grad_ref[:, cols] for cols in head_slices(first, width)], axis=0
        )
        score = lax.dot_general(keys[c], query_rows, CONTRACT_LAST, preferred_element_type=F32)
        dprob = lax.dot_general(values[c], grad_rows, CONTRACT_LAST, preferred_element_type=F32)
        return query_rows, grad_rows, score, dprob

    def softmax(score, dprob):
        expo = jnp.exp2(score * (scale * LOG2_E))
        expo = jnp.concatenate(
            [jnp.where(visible, expo[:prefix], 0.0), jnp.where(causal, expo[prefix:], 0.0)], axis=0
        )
        inverse_sum = 1.0 / jnp.sum(expo, axis=0, keepdims=True)
        delta = jnp.sum(expo * dprob, axis=0, keepdims=True) * inverse_sum
        prob = expo * jnp.where(valid, inverse_sum, 0.0)
        return prob.astype(BF16), (prob * (dprob - delta)).astype(BF16)

    def some_heads(p, _):
        firsts = [c * group + p * HEADS_AT_ONCE for c in range(kv_heads)]
        blocks = [products(c, first) for c, first in enumerate(firsts)]
        probs = [softmax(*block[2:]) for block in blocks]
        query_grads = []
        for c, (prob, dscore) in enumerate(probs):
            query_rows, grad_rows = blocks[c][:2]
            key_sum[c] += jnp.dot(dscore, query_rows, preferred_element_type=F32)
            value_sum[c] += jnp.dot(prob, grad_rows, preferred_element_type=F32)
            query_grads.append(
                lax.dot_general(dscore, keys[c], CONTRACT_FIRST, preferred_element_type=F32)
            )
        for first, query_grad in zip(firsts, query_grads):
            for i, cols in enumerate(head_slices(first, width)):
                unit, inverse = unit_rows(raw_query_ref[:, cols])
                raw_grad, term = norm_rope_back(
                    query_grad[i * length : (i + 1) * length], unit, inverse, query_gain,
                    back_cos, back_sin,
                )
                query_out[:, cols] = raw_grad
                query_terms[...] += fold(term)
            query_copy(first).start()
        return 0

    lax.fori_loop(0, group // HEADS_AT_ONCE, some_heads, 0, unroll=UNROLL)
    for c in range(kv_heads):
        own_cols = slice(c * width, (c + 1) * width)
        unit, inverse = unit_rows(raw_key_ref[:, own_cols])
        raw_grad, term = norm_rope_back(
            key_sum[c, prefix:, :], unit, inverse, key_gain, back_cos, back_sin
        )
        key_out[:, own_cols] = raw_grad
        value_out[:, own_cols] = value_sum[c, prefix:, :]
        key_terms[...] += fold(term)
    last_copies = [
        pltpu.make_async_copy(key_out, key_hbm, sems.at[kv_heads * group // HEADS_AT_ONCE]),
        pltpu.make_async_copy(value_out, value_hbm, sems.at[kv_heads * group // HEADS_AT_ONCE + 1]),
    ]
    for copy in last_copies:
        copy.start()
    for c in range(kv_heads):
        raw_grad, term = norm_rope_back(
            key_sum[c, :prefix, :], *units[c], key_gain, pre_cos * scale, pre_sin * scale
        )
        blocks_out[:, c * width : (c + 1) * width] = raw_grad.astype(BF16)
        blocks_out[:, kv_cols + c * width : kv_cols + (c + 1) * width] = value_sum[
            c, :prefix, :
        ].astype(BF16)
        key_terms[...] += fold(term)
    reward = jnp.full((1, width), reward_ref[0, 0], F32)
    rows = split_terms(jnp.sum(query_terms[...], axis=0, keepdims=True), 2)
    rows += split_terms(jnp.sum(key_terms[...], axis=0, keepdims=True), 2)
    rows += split_terms(reward, 3)
    rows = jnp.concatenate(rows + [jnp.zeros((own - len(rows), width), F32)], axis=0)
    pair = jnp.concatenate([rows, rows], axis=0).astype(BF16)
    for i in range(responses // 2):
        blocks_out[2 * own * i : 2 * own * (i + 1), 2 * kv_cols :] = pair
    for copy in [query_copy(h) for h in range(0, kv_heads * group, HEADS_AT_ONCE)] + last_copies:
        copy.wait()


def advantages(tail, responses):
    tail = tail.astype(F32).reshape(responses, -1, tail.shape[1])
    row = lax.broadcasted_iota(jnp.int32, tail.shape, 1)
    reward = jnp.sum(jnp.where((row >= 4) & (row < 7), tail, 0.0), axis=1, keepdims=True)
    mean = jnp.sum(reward, axis=0, keepdims=True) / responses
    return tail, jnp.broadcast_to(reward - mean, tail.shape), mean[0]


def weigh(blocks_ref, gains_out, *, responses):
    width = gains_out.shape[1]
    tail, weights, _ = advantages(blocks_ref[:, blocks_ref.shape[1] - width :], responses)
    terms = jnp.sum(tail * weights, axis=0)
    query, key = terms[0:1] + terms[1:2], terms[2:3] + terms[3:4]
    row = lax.broadcasted_iota(jnp.int32, gains_out.shape, 0)
    gains_out[...] = jnp.where(row % 2 == 0, query, key)


def finish(
    reward_ref, blocks_ref, query_ref, key_ref, value_ref,
    query_out, key_out, value_out, prefix_key_out, prefix_value_out, *, responses,
):
    own, kv_cols = prefix_key_out.shape
    width = blocks_ref.shape[1] - 2 * kv_cols
    _, weights, mean = advantages(blocks_ref[:, 2 * kv_cols :], responses)
    for out, first in ((prefix_key_out, 0), (prefix_value_out, kv_cols)):
        for cols in range(0, kv_cols, width):
            block = blocks_ref[:, first + cols : first + cols + width].astype(F32)
            out[:, cols : cols + width] = jnp.sum(block.reshape(weights.shape) * weights, axis=0)
    weight = (reward_ref[0, 0] - mean)[:, :1]
    for source, out in ((query_ref, query_out), (key_ref, key_out), (value_ref, value_out)):
        out[...] = (source[...] * weight).astype(BF16)


def local(
    query_raw, response_key_input, response_value_input, prompt_key_input, prompt_value_input,
    query_gain, key_gain, grad_out, rewards, resp_len, prompt_len,
):
    length = query_raw.shape[2]
    width = query_gain.shape[0]
    kv_cols = response_key_input.shape[3]
    kv_heads = kv_cols // width
    query_heads = query_raw.shape[3] // width
    responses = lax.axis_size("resp")
    own = prompt_key_input.shape[1]
    prefix = own * responses
    slot_cols = 2 * kv_cols + width
    table = jnp.asarray(rope_tables(prefix + length, width))
    gains = (query_gain.reshape(1, width), key_gain.reshape(1, width))
    query, key, value, grad = (
        a[0, 0] for a in (query_raw, response_key_input, response_value_input, grad_out)
    )
    shape = jax.ShapeDtypeStruct

    slots = pl.pallas_call(
        send_prompt,
        out_shape=pltpu.VMEM((prefix, 2 * kv_cols), BF16),
        in_specs=[VMEM] * 2,
        out_specs=VMEM,
        name="send_prompt",
    )(prompt_key_input[0], prompt_value_input[0])
    arrived = lax.all_to_all(slots.reshape(responses, own, 2 * kv_cols), "resp", 0, 0)
    prepared = pl.pallas_call(
        prepare,
        out_shape=(
            pltpu.VMEM((query_heads * length, width), BF16),
            pltpu.VMEM((kv_heads * length, width), BF16),
            pltpu.VMEM((table.shape[0] + 8, width), F32),
        ),
        in_specs=[SMEM] + [VMEM] * 5,
        out_specs=(VMEM,) * 3,
        cost_estimate=pl.CostEstimate(
            flops=100_000_000, bytes_accessed=4_000_000, transcendentals=0
        ),
        name="prepare",
    )(prompt_len, query, key, *gains, table)
    *grads, blocks = pl.pallas_call(
        functools.partial(attend, responses=responses),
        out_shape=(
            pltpu.HBM(query.shape, F32),
            pltpu.HBM(key.shape, F32),
            pltpu.HBM(key.shape, F32),
            pltpu.VMEM((prefix, slot_cols), BF16),
        ),
        in_specs=[SMEM] * 3 + [VMEM] * 8,
        out_specs=(pl.BlockSpec(memory_space=pltpu.HBM),) * 3 + (VMEM,),
        scratch_shapes=[
            pltpu.VMEM((kv_heads, prefix + length, width), BF16),
            pltpu.VMEM((kv_heads, prefix + length, width), BF16),
            pltpu.VMEM((kv_heads, prefix + length, width), F32),
            pltpu.VMEM((kv_heads, prefix + length, width), F32),
            pltpu.VMEM((8, width), F32),
            pltpu.VMEM((8, width), F32),
            pltpu.VMEM(query.shape, F32),
            pltpu.VMEM(key.shape, F32),
            pltpu.VMEM(key.shape, F32),
            pltpu.SemaphoreType.DMA((query_heads // HEADS_AT_ONCE + 2,)),
        ],
        compiler_params=pltpu.CompilerParams(vmem_limit_bytes=16 * 2**20),
        name="attend",
    )(
        rewards, resp_len, prompt_len, arrived.reshape(prefix, 2 * kv_cols), *prepared,
        query, key, value, grad,
    )
    received = lax.all_to_all(blocks.reshape(responses, own, slot_cols), "resp", 0, 0)
    received = pltpu.with_memory_space_constraint(
        received.reshape(prefix, slot_cols), pltpu.VMEM
    )
    others = lax.axis_size("dp") * lax.axis_size("tensor")
    gain_slots = pl.pallas_call(
        functools.partial(weigh, responses=responses),
        out_shape=pltpu.VMEM((others * 2, width), F32),
        in_specs=[VMEM],
        out_specs=VMEM,
        name="weigh",
    )(received)
    gain_slots = lax.all_to_all(gain_slots.reshape(others, 2, width), ("dp", "tensor"), 0, 0)
    grad_query, grad_key, grad_value, prefix_key, prefix_value = pl.pallas_call(
        functools.partial(finish, responses=responses),
        out_shape=(
            shape(query.shape, BF16),
            shape(key.shape, BF16),
            shape(key.shape, BF16),
            shape((own, kv_cols), F32),
            shape((own, kv_cols), F32),
        ),
        in_specs=[SMEM] + [VMEM] * 4,
        out_specs=(VMEM,) * 5,
        cost_estimate=pl.CostEstimate(
            flops=10_000_000, bytes_accessed=4_000_000, transcendentals=0
        ),
        name="finish",
    )(rewards, received, *grads)
    totals = jnp.sum(gain_slots, axis=0) / (lax.axis_size("dp") * responses)
    return (
        grad_query[None, None],
        grad_key[None, None],
        grad_value[None, None],
        prefix_key[None],
        prefix_value[None],
        totals[0],
        totals[1],
    )


def solution(mesh):
    token_spec = P("dp", "resp", None, "tensor")
    prompt_spec = P("dp", "resp", "tensor")
    return jax.shard_map(
        local,
        mesh=mesh,
        in_specs=(token_spec,) * 3 + (prompt_spec,) * 2 + (P(), P(), token_spec)
        + (P("dp", "resp"), P("dp", "resp"), P("dp")),
        out_specs=(token_spec,) * 3 + (prompt_spec,) * 2 + (P(), P()),
        check_vma=False,
    )
```

```python
import functools
import math

import jax
import jax.numpy as jnp
import numpy as np
from jax import lax
from jax.experimental import pallas as pl
from jax.experimental.pallas import tpu as pltpu
from jax.sharding import PartitionSpec as P

EPSILON = 1e-06
THETA = 1000000.0
LOG2_E = math.log2(math.e)
F32, BF16 = jnp.float32, jnp.bfloat16
SMEM = pl.BlockSpec(memory_space=pltpu.SMEM)
VMEM = pl.BlockSpec(memory_space=pltpu.VMEM)
CONTRACT_LAST = (((1,), (1,)), ((), ()))
CONTRACT_FIRST = (((0,), (0,)), ((), ()))
HEADS_AT_ONCE = 2
STEP = 16
UNROLL = 2


def rope_tables(positions, width):
    half = width // 2
    inv_freq = (THETA ** (-(np.arange(half) * 2.0) / width)).astype(np.float32)
    rows = [np.arange(STEP), np.arange(0, positions, STEP)]
    angles = [r[:, None].astype(np.float64) * inv_freq for r in rows]
    sign = np.repeat([-1.0, 1.0], half)
    found = []
    for angle in angles:
        angle = np.concatenate([angle, angle], axis=1)
        found += [np.cos(angle), np.sin(angle) * sign]
    return np.concatenate(found, axis=0).astype(np.float32)


def add_angles(one, other):
    return one[0] * other[0] - one[1] * other[1], one[1] * other[0] + one[0] * other[1]


def rope_at(table_ref, start, count):
    steps = (table_ref.shape[0] - 2 * STEP) // 2
    low = (table_ref[:STEP, :], table_ref[STEP : 2 * STEP, :])

    def high(m):
        first = 2 * STEP + m
        return table_ref[pl.ds(first, 1), :], table_ref[pl.ds(first + steps, 1), :]

    if not isinstance(start, int):
        within = start % STEP
        row = (table_ref[pl.ds(within, 1), :], table_ref[pl.ds(STEP + within, 1), :])
        low = add_angles(low, add_angles(high(start // STEP), row))
    blocks = [add_angles(low, high(m)) for m in range(count // STEP)]
    return tuple(jnp.concatenate([block[i] for block in blocks], axis=0) for i in range(2))


def half_turn(rows):
    return pltpu.roll(rows, rows.shape[1] // 2, 1)


def unit_rows(raw):
    raw = raw.astype(F32)
    inverse = lax.rsqrt(jnp.mean(raw * raw, axis=1, keepdims=True) + EPSILON)
    return raw * inverse, inverse


def rotated(unit, gain, cos, sin):
    normed = unit * gain
    return (normed * cos + half_turn(normed) * sin).astype(BF16)


def norm_rope_back(grad, unit, inverse, gain, cos, sin):
    normed_grad = grad * cos - half_turn(grad) * sin
    term = normed_grad * unit
    mean = jnp.mean(term * gain, axis=1, keepdims=True)
    return inverse * (normed_grad * gain - unit * mean), term


def fold(rows):
    return jnp.sum(rows.reshape(-1, 8, rows.shape[1]), axis=0)


def split_terms(value, terms):
    found = []
    for _ in range(terms):
        found.append(value.astype(BF16).astype(F32))
        value = value - found[-1]
    return found


def send_prompt(key_ref, value_ref, out_ref):
    own = key_ref.shape[0]
    slot = jnp.concatenate([key_ref[...], value_ref[...]], axis=1).astype(F32)
    slots = jnp.concatenate([slot, slot], axis=0).astype(BF16)
    for i in range(out_ref.shape[0] // (2 * own)):
        out_ref[2 * own * i : 2 * own * (i + 1), :] = slots


def head_slices(first, width):
    return [
        pl.ds(pl.multiple_of((first + i) * width, width), width) for i in range(HEADS_AT_ONCE)
    ]


def prepare(
    prompt_len_ref, query_ref, key_ref, query_gain_ref, key_gain_ref, table_ref,
    query_out, key_out, shared_out,
):
    length, width = query_ref.shape[0], query_gain_ref.shape[1]
    cos, sin = rope_at(table_ref, prompt_len_ref[0], length)
    shared_out[: table_ref.shape[0], :] = table_ref[...]
    shared_out[table_ref.shape[0] :, :] = jnp.concatenate(
        [query_gain_ref[...], key_gain_ref[...], jnp.zeros((6, width), F32)], axis=0
    )
    for source, gain_ref, out in (
        (key_ref, key_gain_ref, key_out),
        (query_ref, query_gain_ref, query_out),
    ):
        gain = gain_ref[...]

        def one(h, _, source=source, gain=gain, out=out):
            raw = source[:, pl.ds(pl.multiple_of(h * width, width), width)]
            rows = rotated(unit_rows(raw)[0], gain, cos, sin)
            out[pl.ds(pl.multiple_of(h * length, length), length), :] = rows
            return 0

        lax.fori_loop(0, source.shape[1] // width, one, 0, unroll=2)


def attend(
    reward_ref, resp_len_ref, prompt_len_ref,
    arrived_ref, query_ref, key_ref, shared_ref, raw_query_ref, raw_key_ref, value_ref, grad_ref,
    query_hbm, last_out, key_out, value_out, blocks_out,
    keys, values, key_sum, value_sum, query_terms, key_terms, query_out, sems, *, responses,
):
    length, width = grad_ref.shape[0], shared_ref.shape[1]
    prefix = arrived_ref.shape[0]
    kv_heads = raw_key_ref.shape[1] // width
    kv_cols = kv_heads * width
    group = grad_ref.shape[1] // kv_cols
    own = prefix // responses
    count = HEADS_AT_ONCE * length
    scale = width**-0.5
    start = prompt_len_ref[0]
    table_ref = shared_ref.at[: shared_ref.shape[0] - 8]
    query_gain, key_gain = (shared_ref[pl.ds(shared_ref.shape[0] - 8 + i, 1), :] for i in range(2))
    back_cos, back_sin = (t * scale for t in rope_at(table_ref, start, length))
    pre_cos, pre_sin = rope_at(table_ref, 0, prefix)

    valid = lax.broadcasted_iota(jnp.int32, (1, count), 1) % length < resp_len_ref[0, 0]
    visible = lax.broadcasted_iota(jnp.int32, (prefix, count), 0) < start
    causal = lax.broadcasted_iota(jnp.int32, (length, count), 0) <= (
        lax.broadcasted_iota(jnp.int32, (length, count), 1) % length
    )
    query_terms[...] = jnp.zeros_like(query_terms)
    key_terms[...] = jnp.zeros_like(key_terms)

    steps = group // HEADS_AT_ONCE
    step_cols = HEADS_AT_ONCE * width

    def query_copy(c, p):
        source = pl.ds(pl.multiple_of((c * steps + p) * step_cols, step_cols), step_cols)
        target = pl.ds(pl.multiple_of((c * (steps - 1) + p) * step_cols, step_cols), step_cols)
        return pltpu.make_async_copy(
            query_out.at[:, source], query_hbm.at[:, target], sems.at[c * (steps - 1) + p]
        )

    units = []
    for c in range(kv_heads):
        unit = unit_rows(arrived_ref[:, c * width : (c + 1) * width])
        units.append(unit)
        keys[c, :prefix, :] = rotated(unit[0], key_gain, pre_cos, pre_sin)
        keys[c, prefix:, :] = key_ref[c * length : (c + 1) * length, :]
        values[c, :prefix, :] = arrived_ref[:, kv_cols + c * width : kv_cols + (c + 1) * width]
        values[c, prefix:, :] = value_ref[:, c * width : (c + 1) * width]
    key_sum[...] = jnp.zeros_like(key_sum)
    value_sum[...] = jnp.zeros_like(value_sum)

    def products(c, first):
        span = pl.ds(pl.multiple_of(first * length, length), count)
        query_rows = query_ref[span, :]
        grad_rows = jnp.concatenate(
            [grad_ref[:, cols] for cols in head_slices(first, width)], axis=0
        )
        score = lax.dot_general(keys[c], query_rows, CONTRACT_LAST, preferred_element_type=F32)
        dprob = lax.dot_general(values[c], grad_rows, CONTRACT_LAST, preferred_element_type=F32)
        return query_rows, grad_rows, score, dprob

    def softmax(score, dprob):
        expo = jnp.exp2(score * (scale * LOG2_E))
        expo = jnp.concatenate(
            [jnp.where(visible, expo[:prefix], 0.0), jnp.where(causal, expo[prefix:], 0.0)], axis=0
        )
        inverse_sum = 1.0 / jnp.sum(expo, axis=0, keepdims=True)
        delta = jnp.sum(expo * dprob, axis=0, keepdims=True) * inverse_sum
        prob = expo * jnp.where(valid, inverse_sum, 0.0)
        return prob.astype(BF16), (prob * (dprob - delta)).astype(BF16)

    def some_heads(p, _):
        firsts = [c * group + p * HEADS_AT_ONCE for c in range(kv_heads)]
        blocks = [products(c, first) for c, first in enumerate(firsts)]
        probs = [softmax(*block[2:]) for block in blocks]
        query_grads = []
        for c, (prob, dscore) in enumerate(probs):
            query_rows, grad_rows = blocks[c][:2]
            key_sum[c] += jnp.dot(dscore, query_rows, preferred_element_type=F32)
            value_sum[c] += jnp.dot(prob, grad_rows, preferred_element_type=F32)
            query_grads.append(
                lax.dot_general(dscore, keys[c], CONTRACT_FIRST, preferred_element_type=F32)
            )
        for c, (first, query_grad) in enumerate(zip(firsts, query_grads)):
            for i, cols in enumerate(head_slices(first, width)):
                unit, inverse = unit_rows(raw_query_ref[:, cols])
                raw_grad, term = norm_rope_back(
                    query_grad[i * length : (i + 1) * length], unit, inverse, query_gain,
                    back_cos, back_sin,
                )
                query_out[:, cols] = raw_grad
                query_terms[...] += fold(term)

            @pl.when(p < steps - 1)
            def _(c=c):
                query_copy(c, p).start()

        return 0

    lax.fori_loop(0, steps, some_heads, 0, unroll=UNROLL)
    for c in range(kv_heads):
        own_cols = slice(c * width, (c + 1) * width)
        unit, inverse = unit_rows(raw_key_ref[:, own_cols])
        raw_grad, term = norm_rope_back(
            key_sum[c, prefix:, :], unit, inverse, key_gain, back_cos, back_sin
        )
        key_out[:, own_cols] = raw_grad
        value_out[:, own_cols] = value_sum[c, prefix:, :]
        key_terms[...] += fold(term)
    for c in range(kv_heads):
        cols = slice(((c + 1) * steps - 1) * step_cols, (c + 1) * steps * step_cols)
        last_out[:, c * step_cols : (c + 1) * step_cols] = query_out[:, cols]
    for c in range(kv_heads):
        raw_grad, term = norm_rope_back(
            key_sum[c, :prefix, :], *units[c], key_gain, pre_cos * scale, pre_sin * scale
        )
        blocks_out[:, c * width : (c + 1) * width] = raw_grad.astype(BF16)
        blocks_out[:, kv_cols + c * width : kv_cols + (c + 1) * width] = value_sum[
            c, :prefix, :
        ].astype(BF16)
        key_terms[...] += fold(term)
    reward = jnp.full((1, width), reward_ref[0, 0], F32)
    rows = split_terms(jnp.sum(query_terms[...], axis=0, keepdims=True), 2)
    rows += split_terms(jnp.sum(key_terms[...], axis=0, keepdims=True), 2)
    rows += split_terms(reward, 3)
    rows = jnp.concatenate(rows + [jnp.zeros((own - len(rows), width), F32)], axis=0)
    pair = jnp.concatenate([rows, rows], axis=0).astype(BF16)
    for i in range(responses // 2):
        blocks_out[2 * own * i : 2 * own * (i + 1), 2 * kv_cols :] = pair
    for c in range(kv_heads):
        for p in range(steps - 1):
            query_copy(c, p).wait()


def advantages(tail, responses):
    tail = tail.astype(F32).reshape(responses, -1, tail.shape[1])
    row = lax.broadcasted_iota(jnp.int32, tail.shape, 1)
    reward = jnp.sum(jnp.where((row >= 4) & (row < 7), tail, 0.0), axis=1, keepdims=True)
    mean = jnp.sum(reward, axis=0, keepdims=True) / responses
    return tail, jnp.broadcast_to(reward - mean, tail.shape), mean[0]


def weigh(blocks_ref, gains_out, *, responses):
    width = gains_out.shape[1]
    tail, weights, _ = advantages(blocks_ref[:, blocks_ref.shape[1] - width :], responses)
    terms = jnp.sum(tail * weights, axis=0)
    query, key = terms[0:1] + terms[1:2], terms[2:3] + terms[3:4]
    row = lax.broadcasted_iota(jnp.int32, gains_out.shape, 0)
    gains_out[...] = jnp.where(row % 2 == 0, query, key)


def finish(
    reward_ref, blocks_ref, query_ref, last_ref, key_ref, value_ref,
    query_out, key_out, value_out, prefix_key_out, prefix_value_out, *, responses,
):
    own, kv_cols = prefix_key_out.shape
    width = blocks_ref.shape[1] - 2 * kv_cols
    _, weights, mean = advantages(blocks_ref[:, 2 * kv_cols :], responses)
    for out, first in ((prefix_key_out, 0), (prefix_value_out, kv_cols)):
        for cols in range(0, kv_cols, width):
            block = blocks_ref[:, first + cols : first + cols + width].astype(F32)
            out[:, cols : cols + width] = jnp.sum(block.reshape(weights.shape) * weights, axis=0)
    weight = (reward_ref[0, 0] - mean)[:, :1]
    for source, out in ((key_ref, key_out), (value_ref, value_out)):
        out[...] = (source[...] * weight).astype(BF16)
    kv_heads = kv_cols // width
    early, late = query_ref.shape[1] // kv_heads, last_ref.shape[1] // kv_heads
    for c in range(kv_heads):
        first = c * (early + late)
        for source, begin, cols in ((query_ref, first, early), (last_ref, first + early, late)):
            grad = source[:, c * cols : (c + 1) * cols]
            query_out[:, begin : begin + cols] = (grad * weight).astype(BF16)


def local(
    query_raw, response_key_input, response_value_input, prompt_key_input, prompt_value_input,
    query_gain, key_gain, grad_out, rewards, resp_len, prompt_len,
):
    length = query_raw.shape[2]
    width = query_gain.shape[0]
    kv_cols = response_key_input.shape[3]
    kv_heads = kv_cols // width
    query_heads = query_raw.shape[3] // width
    responses = lax.axis_size("resp")
    own = prompt_key_input.shape[1]
    prefix = own * responses
    slot_cols = 2 * kv_cols + width
    table = jnp.asarray(rope_tables(prefix + length, width))
    gains = (query_gain.reshape(1, width), key_gain.reshape(1, width))
    query, key, value, grad = (
        a[0, 0] for a in (query_raw, response_key_input, response_value_input, grad_out)
    )
    shape = jax.ShapeDtypeStruct

    slots = pl.pallas_call(
        send_prompt,
        out_shape=pltpu.VMEM((prefix, 2 * kv_cols), BF16),
        in_specs=[VMEM] * 2,
        out_specs=VMEM,
        name="send_prompt",
    )(prompt_key_input[0], prompt_value_input[0])
    arrived = lax.all_to_all(slots.reshape(responses, own, 2 * kv_cols), "resp", 0, 0)
    prepared = pl.pallas_call(
        prepare,
        out_shape=(
            pltpu.VMEM((query_heads * length, width), BF16),
            pltpu.VMEM((kv_heads * length, width), BF16),
            pltpu.VMEM((table.shape[0] + 8, width), F32),
        ),
        in_specs=[SMEM] + [VMEM] * 5,
        out_specs=(VMEM,) * 3,
        cost_estimate=pl.CostEstimate(
            flops=100_000_000, bytes_accessed=4_000_000, transcendentals=0
        ),
        name="prepare",
    )(prompt_len, query, key, *gains, table)
    last_cols = kv_heads * HEADS_AT_ONCE * width
    *grads, blocks = pl.pallas_call(
        functools.partial(attend, responses=responses),
        out_shape=(
            pltpu.HBM((length, query.shape[1] - last_cols), F32),
            pltpu.VMEM((length, last_cols), F32),
            pltpu.VMEM(key.shape, F32),
            pltpu.VMEM(key.shape, F32),
            pltpu.VMEM((prefix, slot_cols), BF16),
        ),
        in_specs=[SMEM] * 3 + [VMEM] * 8,
        out_specs=(pl.BlockSpec(memory_space=pltpu.HBM),) + (VMEM,) * 4,
        scratch_shapes=[
            pltpu.VMEM((kv_heads, prefix + length, width), BF16),
            pltpu.VMEM((kv_heads, prefix + length, width), BF16),
            pltpu.VMEM((kv_heads, prefix + length, width), F32),
            pltpu.VMEM((kv_heads, prefix + length, width), F32),
            pltpu.VMEM((8, width), F32),
            pltpu.VMEM((8, width), F32),
            pltpu.VMEM(query.shape, F32),
            pltpu.SemaphoreType.DMA((query_heads // HEADS_AT_ONCE - kv_heads,)),
        ],
        compiler_params=pltpu.CompilerParams(vmem_limit_bytes=16 * 2**20),
        name="attend",
    )(
        rewards, resp_len, prompt_len, arrived.reshape(prefix, 2 * kv_cols), *prepared,
        query, key, value, grad,
    )
    received = lax.all_to_all(blocks.reshape(responses, own, slot_cols), "resp", 0, 0)
    received = pltpu.with_memory_space_constraint(
        received.reshape(prefix, slot_cols), pltpu.VMEM
    )
    others = lax.axis_size("dp") * lax.axis_size("tensor")
    gain_slots = pl.pallas_call(
        functools.partial(weigh, responses=responses),
        out_shape=pltpu.VMEM((others * 2, width), F32),
        in_specs=[VMEM],
        out_specs=VMEM,
        name="weigh",
    )(received)
    gain_slots = lax.all_to_all(gain_slots.reshape(others, 2, width), ("dp", "tensor"), 0, 0)
    grad_query, grad_key, grad_value, prefix_key, prefix_value = pl.pallas_call(
        functools.partial(finish, responses=responses),
        out_shape=(
            shape(query.shape, BF16),
            shape(key.shape, BF16),
            shape(key.shape, BF16),
            shape((own, kv_cols), F32),
            shape((own, kv_cols), F32),
        ),
        in_specs=[SMEM] + [VMEM] * 5,
        out_specs=(VMEM,) * 5,
        cost_estimate=pl.CostEstimate(
            flops=10_000_000, bytes_accessed=4_000_000, transcendentals=0
        ),
        name="finish",
    )(rewards, received, *grads)
    totals = jnp.sum(gain_slots, axis=0) / (lax.axis_size("dp") * responses)
    return (
        grad_query[None, None],
        grad_key[None, None],
        grad_value[None, None],
        prefix_key[None],
        prefix_value[None],
        totals[0],
        totals[1],
    )


def solution(mesh):
    token_spec = P("dp", "resp", None, "tensor")
    prompt_spec = P("dp", "resp", "tensor")
    return jax.shard_map(
        local,
        mesh=mesh,
        in_specs=(token_spec,) * 3 + (prompt_spec,) * 2 + (P(), P(), token_spec)
        + (P("dp", "resp"), P("dp", "resp"), P("dp")),
        out_specs=(token_spec,) * 3 + (prompt_spec,) * 2 + (P(), P()),
        check_vma=False,
    )
```

```python
import functools
import math

import jax
import jax.numpy as jnp
import numpy as np
from jax import lax
from jax.experimental import pallas as pl
from jax.experimental.pallas import tpu as pltpu
from jax.sharding import PartitionSpec as P

EPSILON = 1e-06
THETA = 1000000.0
LOG2_E = math.log2(math.e)
F32, BF16 = jnp.float32, jnp.bfloat16
SMEM = pl.BlockSpec(memory_space=pltpu.SMEM)
VMEM = pl.BlockSpec(memory_space=pltpu.VMEM)
CONTRACT_LAST = (((1,), (1,)), ((), ()))
CONTRACT_FIRST = (((0,), (0,)), ((), ()))
HEADS_AT_ONCE = 2
STEP = 16
UNROLL = 2


def rope_tables(positions, width):
    half = width // 2
    inv_freq = (THETA ** (-(np.arange(half) * 2.0) / width)).astype(np.float32)
    rows = [np.arange(STEP), np.arange(0, positions, STEP)]
    angles = [r[:, None].astype(np.float64) * inv_freq for r in rows]
    sign = np.repeat([-1.0, 1.0], half)
    found = []
    for angle in angles:
        angle = np.concatenate([angle, angle], axis=1)
        found += [np.cos(angle), np.sin(angle) * sign]
    return np.concatenate(found, axis=0).astype(np.float32)


def add_angles(one, other):
    return one[0] * other[0] - one[1] * other[1], one[1] * other[0] + one[0] * other[1]


def rope_at(table_ref, start, count):
    steps = (table_ref.shape[0] - 2 * STEP) // 2
    low = (table_ref[:STEP, :], table_ref[STEP : 2 * STEP, :])

    def high(m):
        first = 2 * STEP + m
        return table_ref[pl.ds(first, 1), :], table_ref[pl.ds(first + steps, 1), :]

    if not isinstance(start, int):
        within = start % STEP
        row = (table_ref[pl.ds(within, 1), :], table_ref[pl.ds(STEP + within, 1), :])
        low = add_angles(low, add_angles(high(start // STEP), row))
    blocks = [add_angles(low, high(m)) for m in range(count // STEP)]
    return tuple(jnp.concatenate([block[i] for block in blocks], axis=0) for i in range(2))


def half_turn(rows):
    return pltpu.roll(rows, rows.shape[1] // 2, 1)


def unit_rows(raw):
    raw = raw.astype(F32)
    inverse = lax.rsqrt(jnp.mean(raw * raw, axis=1, keepdims=True) + EPSILON)
    return raw * inverse, inverse


def rotated(unit, gain, cos, sin):
    normed = unit * gain
    return (normed * cos + half_turn(normed) * sin).astype(BF16)


def rope_back(grad, cos, sin):
    return grad * cos - half_turn(grad) * sin


def norm_back(normed_grad, term, unit, inverse, gain):
    mean = jnp.mean(term * gain, axis=1, keepdims=True)
    return inverse * (normed_grad * gain - unit * mean)


def norm_rope_back(grad, unit, inverse, gain, cos, sin):
    normed_grad = rope_back(grad, cos, sin)
    term = normed_grad * unit
    return norm_back(normed_grad, term, unit, inverse, gain), term


def fold(rows):
    return jnp.sum(rows.reshape(-1, 8, rows.shape[1]), axis=0)


def split_terms(value, terms):
    found = []
    for _ in range(terms):
        found.append(value.astype(BF16).astype(F32))
        value = value - found[-1]
    return found


def send_prompt(key_ref, value_ref, out_ref):
    own = key_ref.shape[0]
    slot = jnp.concatenate([key_ref[...], value_ref[...]], axis=1).astype(F32)
    slots = jnp.concatenate([slot, slot], axis=0).astype(BF16)
    for i in range(out_ref.shape[0] // (2 * own)):
        out_ref[2 * own * i : 2 * own * (i + 1), :] = slots


def head_slices(first, width):
    return [
        pl.ds(pl.multiple_of((first + i) * width, width), width) for i in range(HEADS_AT_ONCE)
    ]


def prepare(
    prompt_len_ref, query_ref, key_ref, query_gain_ref, key_gain_ref, table_ref,
    query_out, key_out, unit_out, shared_out,
):
    length, width = query_ref.shape[0], query_gain_ref.shape[1]
    cos, sin = rope_at(table_ref, prompt_len_ref[0], length)
    shared_out[: table_ref.shape[0], :] = table_ref[...]
    shared_out[table_ref.shape[0] :, :] = jnp.concatenate(
        [query_gain_ref[...], key_gain_ref[...], jnp.zeros((6, width), F32)], axis=0
    )
    for source, gain_ref, out in (
        (key_ref, key_gain_ref, key_out),
        (query_ref, query_gain_ref, query_out),
    ):
        gain = gain_ref[...]

        def one(h, _, source=source, gain=gain, out=out):
            cols = pl.ds(pl.multiple_of(h * width, width), width)
            unit = unit_rows(source[:, cols])[0]
            if out is query_out:
                unit_out[:, cols] = unit.astype(BF16)
            rows = rotated(unit, gain, cos, sin)
            out[pl.ds(pl.multiple_of(h * length, length), length), :] = rows
            return 0

        lax.fori_loop(0, source.shape[1] // width, one, 0, unroll=2)


def attend(
    reward_ref, resp_len_ref, prompt_len_ref,
    arrived_ref, query_ref, key_ref, unit_ref, shared_ref, raw_key_ref, value_ref, grad_ref,
    query_hbm, last_out, key_out, value_out, blocks_out,
    keys, values, key_sum, value_sum, query_terms, key_terms, query_out, sems, *, responses,
):
    length, width = grad_ref.shape[0], shared_ref.shape[1]
    prefix = arrived_ref.shape[0]
    kv_heads = raw_key_ref.shape[1] // width
    kv_cols = kv_heads * width
    group = grad_ref.shape[1] // kv_cols
    own = prefix // responses
    count = HEADS_AT_ONCE * length
    scale = width**-0.5
    start = prompt_len_ref[0]
    table_ref = shared_ref.at[: shared_ref.shape[0] - 8]
    key_gain = shared_ref[pl.ds(shared_ref.shape[0] - 7, 1), :]
    back_cos, back_sin = (t * scale for t in rope_at(table_ref, start, length))
    pre_cos, pre_sin = rope_at(table_ref, 0, prefix)

    valid = lax.broadcasted_iota(jnp.int32, (1, count), 1) % length < resp_len_ref[0, 0]
    visible = lax.broadcasted_iota(jnp.int32, (prefix, count), 0) < start
    causal = lax.broadcasted_iota(jnp.int32, (length, count), 0) <= (
        lax.broadcasted_iota(jnp.int32, (length, count), 1) % length
    )
    query_terms[...] = jnp.zeros_like(query_terms)
    key_terms[...] = jnp.zeros_like(key_terms)

    steps = group // HEADS_AT_ONCE
    step_cols = HEADS_AT_ONCE * width

    def query_copy(c, p):
        source = pl.ds(pl.multiple_of((c * steps + p) * step_cols, step_cols), step_cols)
        target = pl.ds(pl.multiple_of((c * (steps - 1) + p) * step_cols, step_cols), step_cols)
        return pltpu.make_async_copy(
            query_out.at[:, source], query_hbm.at[:, target], sems.at[c * (steps - 1) + p]
        )

    units = []
    for c in range(kv_heads):
        unit = unit_rows(arrived_ref[:, c * width : (c + 1) * width])
        units.append(unit)
        keys[c, :prefix, :] = rotated(unit[0], key_gain, pre_cos, pre_sin)
        keys[c, prefix:, :] = key_ref[c * length : (c + 1) * length, :]
        values[c, :prefix, :] = arrived_ref[:, kv_cols + c * width : kv_cols + (c + 1) * width]
        values[c, prefix:, :] = value_ref[:, c * width : (c + 1) * width]
    key_sum[...] = jnp.zeros_like(key_sum)
    value_sum[...] = jnp.zeros_like(value_sum)

    def products(c, first):
        span = pl.ds(pl.multiple_of(first * length, length), count)
        query_rows = query_ref[span, :]
        grad_rows = jnp.concatenate(
            [grad_ref[:, cols] for cols in head_slices(first, width)], axis=0
        )
        score = lax.dot_general(keys[c], query_rows, CONTRACT_LAST, preferred_element_type=F32)
        dprob = lax.dot_general(values[c], grad_rows, CONTRACT_LAST, preferred_element_type=F32)
        return query_rows, grad_rows, score, dprob

    def softmax(score, dprob):
        expo = jnp.exp2(score * (scale * LOG2_E))
        expo = jnp.concatenate(
            [jnp.where(visible, expo[:prefix], 0.0), jnp.where(causal, expo[prefix:], 0.0)], axis=0
        )
        inverse_sum = 1.0 / jnp.sum(expo, axis=0, keepdims=True)
        delta = jnp.sum(expo * dprob, axis=0, keepdims=True) * inverse_sum
        prob = expo * jnp.where(valid, inverse_sum, 0.0)
        return prob.astype(BF16), (prob * (dprob - delta)).astype(BF16)

    def some_heads(p, _):
        firsts = [c * group + p * HEADS_AT_ONCE for c in range(kv_heads)]
        blocks = [products(c, first) for c, first in enumerate(firsts)]
        probs = [softmax(*block[2:]) for block in blocks]
        query_grads = []
        for c, (prob, dscore) in enumerate(probs):
            query_rows, grad_rows = blocks[c][:2]
            key_sum[c] += jnp.dot(dscore, query_rows, preferred_element_type=F32)
            value_sum[c] += jnp.dot(prob, grad_rows, preferred_element_type=F32)
            query_grads.append(
                lax.dot_general(dscore, keys[c], CONTRACT_FIRST, preferred_element_type=F32)
            )
        for c, (first, query_grad) in enumerate(zip(firsts, query_grads)):
            for i, cols in enumerate(head_slices(first, width)):
                normed_grad = rope_back(
                    query_grad[i * length : (i + 1) * length], back_cos, back_sin
                )
                query_out[:, cols] = normed_grad
                query_terms[...] += fold(normed_grad * unit_ref[:, cols].astype(F32))

            @pl.when(p < steps - 1)
            def _(c=c):
                query_copy(c, p).start()

        return 0

    lax.fori_loop(0, steps, some_heads, 0, unroll=UNROLL)
    for c in range(kv_heads):
        own_cols = slice(c * width, (c + 1) * width)
        unit, inverse = unit_rows(raw_key_ref[:, own_cols])
        raw_grad, term = norm_rope_back(
            key_sum[c, prefix:, :], unit, inverse, key_gain, back_cos, back_sin
        )
        key_out[:, own_cols] = raw_grad
        value_out[:, own_cols] = value_sum[c, prefix:, :]
        key_terms[...] += fold(term)
    for c in range(kv_heads):
        cols = slice(((c + 1) * steps - 1) * step_cols, (c + 1) * steps * step_cols)
        last_out[:, c * step_cols : (c + 1) * step_cols] = query_out[:, cols]
    for c in range(kv_heads):
        raw_grad, term = norm_rope_back(
            key_sum[c, :prefix, :], *units[c], key_gain, pre_cos * scale, pre_sin * scale
        )
        blocks_out[:, c * width : (c + 1) * width] = raw_grad.astype(BF16)
        blocks_out[:, kv_cols + c * width : kv_cols + (c + 1) * width] = value_sum[
            c, :prefix, :
        ].astype(BF16)
        key_terms[...] += fold(term)
    reward = jnp.full((1, width), reward_ref[0, 0], F32)
    rows = split_terms(jnp.sum(query_terms[...], axis=0, keepdims=True), 2)
    rows += split_terms(jnp.sum(key_terms[...], axis=0, keepdims=True), 2)
    rows += split_terms(reward, 3)
    rows = jnp.concatenate(rows + [jnp.zeros((own - len(rows), width), F32)], axis=0)
    pair = jnp.concatenate([rows, rows], axis=0).astype(BF16)
    for i in range(responses // 2):
        blocks_out[2 * own * i : 2 * own * (i + 1), 2 * kv_cols :] = pair
    for c in range(kv_heads):
        for p in range(steps - 1):
            query_copy(c, p).wait()


def advantages(tail, responses):
    tail = tail.astype(F32).reshape(responses, -1, tail.shape[1])
    row = lax.broadcasted_iota(jnp.int32, tail.shape, 1)
    reward = jnp.sum(jnp.where((row >= 4) & (row < 7), tail, 0.0), axis=1, keepdims=True)
    mean = jnp.sum(reward, axis=0, keepdims=True) / responses
    return tail, jnp.broadcast_to(reward - mean, tail.shape), mean[0]


def weigh(blocks_ref, gains_out, *, responses):
    width = gains_out.shape[1]
    tail, weights, _ = advantages(blocks_ref[:, blocks_ref.shape[1] - width :], responses)
    terms = jnp.sum(tail * weights, axis=0)
    query, key = terms[0:1] + terms[1:2], terms[2:3] + terms[3:4]
    row = lax.broadcasted_iota(jnp.int32, gains_out.shape, 0)
    gains_out[...] = jnp.where(row % 2 == 0, query, key)


def finish(
    reward_ref, blocks_ref, raw_query_ref, query_gain_ref, query_ref, last_ref, key_ref, value_ref,
    query_out, key_out, value_out, prefix_key_out, prefix_value_out, *, responses,
):
    own, kv_cols = prefix_key_out.shape
    width = blocks_ref.shape[1] - 2 * kv_cols
    _, weights, mean = advantages(blocks_ref[:, 2 * kv_cols :], responses)
    for out, first in ((prefix_key_out, 0), (prefix_value_out, kv_cols)):
        for cols in range(0, kv_cols, width):
            block = blocks_ref[:, first + cols : first + cols + width].astype(F32)
            out[:, cols : cols + width] = jnp.sum(block.reshape(weights.shape) * weights, axis=0)
    weight = (reward_ref[0, 0] - mean)[:, :1]
    for source, out in ((key_ref, key_out), (value_ref, value_out)):
        out[...] = (source[...] * weight).astype(BF16)
    kv_heads = kv_cols // width
    early, late = query_ref.shape[1] // kv_heads, last_ref.shape[1] // kv_heads
    for c in range(kv_heads):
        first = c * (early + late)
        for source, begin, cols in ((query_ref, first, early), (last_ref, first + early, late)):

            def one(h, _, source=source, begin=begin, skip=c * cols):
                at = [pl.ds(pl.multiple_of(x + h * width, width), width) for x in (begin, skip)]
                normed_grad = source[:, at[1]]
                unit, inverse = unit_rows(raw_query_ref[:, at[0]])
                grad = norm_back(
                    normed_grad, normed_grad * unit, unit, inverse, query_gain_ref[...]
                )
                query_out[:, at[0]] = (grad * weight).astype(BF16)
                return 0

            lax.fori_loop(0, cols // width, one, 0, unroll=2)


def local(
    query_raw, response_key_input, response_value_input, prompt_key_input, prompt_value_input,
    query_gain, key_gain, grad_out, rewards, resp_len, prompt_len,
):
    length = query_raw.shape[2]
    width = query_gain.shape[0]
    kv_cols = response_key_input.shape[3]
    kv_heads = kv_cols // width
    query_heads = query_raw.shape[3] // width
    responses = lax.axis_size("resp")
    own = prompt_key_input.shape[1]
    prefix = own * responses
    slot_cols = 2 * kv_cols + width
    table = jnp.asarray(rope_tables(prefix + length, width))
    gains = (query_gain.reshape(1, width), key_gain.reshape(1, width))
    query, key, value, grad = (
        a[0, 0] for a in (query_raw, response_key_input, response_value_input, grad_out)
    )
    shape = jax.ShapeDtypeStruct

    slots = pl.pallas_call(
        send_prompt,
        out_shape=pltpu.VMEM((prefix, 2 * kv_cols), BF16),
        in_specs=[VMEM] * 2,
        out_specs=VMEM,
        name="send_prompt",
    )(prompt_key_input[0], prompt_value_input[0])
    arrived = lax.all_to_all(slots.reshape(responses, own, 2 * kv_cols), "resp", 0, 0)
    prepared = pl.pallas_call(
        prepare,
        out_shape=(
            pltpu.VMEM((query_heads * length, width), BF16),
            pltpu.VMEM((kv_heads * length, width), BF16),
            pltpu.VMEM(query.shape, BF16),
            pltpu.VMEM((table.shape[0] + 8, width), F32),
        ),
        in_specs=[SMEM] + [VMEM] * 5,
        out_specs=(VMEM,) * 4,
        cost_estimate=pl.CostEstimate(
            flops=100_000_000, bytes_accessed=4_000_000, transcendentals=0
        ),
        name="prepare",
    )(prompt_len, query, key, *gains, table)
    last_cols = kv_heads * HEADS_AT_ONCE * width
    *grads, blocks = pl.pallas_call(
        functools.partial(attend, responses=responses),
        out_shape=(
            pltpu.HBM((length, query.shape[1] - last_cols), F32),
            pltpu.VMEM((length, last_cols), F32),
            pltpu.VMEM(key.shape, F32),
            pltpu.VMEM(key.shape, F32),
            pltpu.VMEM((prefix, slot_cols), BF16),
        ),
        in_specs=[SMEM] * 3 + [VMEM] * 8,
        out_specs=(pl.BlockSpec(memory_space=pltpu.HBM),) + (VMEM,) * 4,
        scratch_shapes=[
            pltpu.VMEM((kv_heads, prefix + length, width), BF16),
            pltpu.VMEM((kv_heads, prefix + length, width), BF16),
            pltpu.VMEM((kv_heads, prefix + length, width), F32),
            pltpu.VMEM((kv_heads, prefix + length, width), F32),
            pltpu.VMEM((8, width), F32),
            pltpu.VMEM((8, width), F32),
            pltpu.VMEM(query.shape, F32),
            pltpu.SemaphoreType.DMA((query_heads // HEADS_AT_ONCE - kv_heads,)),
        ],
        compiler_params=pltpu.CompilerParams(vmem_limit_bytes=16 * 2**20),
        name="attend",
    )(
        rewards, resp_len, prompt_len, arrived.reshape(prefix, 2 * kv_cols), *prepared,
        key, value, grad,
    )
    received = lax.all_to_all(blocks.reshape(responses, own, slot_cols), "resp", 0, 0)
    received = pltpu.with_memory_space_constraint(
        received.reshape(prefix, slot_cols), pltpu.VMEM
    )
    others = lax.axis_size("dp") * lax.axis_size("tensor")
    gain_slots = pl.pallas_call(
        functools.partial(weigh, responses=responses),
        out_shape=pltpu.VMEM((others * 2, width), F32),
        in_specs=[VMEM],
        out_specs=VMEM,
        name="weigh",
    )(received)
    gain_slots = lax.all_to_all(gain_slots.reshape(others, 2, width), ("dp", "tensor"), 0, 0)
    grad_query, grad_key, grad_value, prefix_key, prefix_value = pl.pallas_call(
        functools.partial(finish, responses=responses),
        out_shape=(
            shape(query.shape, BF16),
            shape(key.shape, BF16),
            shape(key.shape, BF16),
            shape((own, kv_cols), F32),
            shape((own, kv_cols), F32),
        ),
        in_specs=[SMEM] + [VMEM] * 7,
        out_specs=(VMEM,) * 5,
        cost_estimate=pl.CostEstimate(
            flops=10_000_000, bytes_accessed=4_000_000, transcendentals=0
        ),
        name="finish",
    )(rewards, received, query, gains[0], *grads)
    totals = jnp.sum(gain_slots, axis=0) / (lax.axis_size("dp") * responses)
    return (
        grad_query[None, None],
        grad_key[None, None],
        grad_value[None, None],
        prefix_key[None],
        prefix_value[None],
        totals[0],
        totals[1],
    )


def solution(mesh):
    token_spec = P("dp", "resp", None, "tensor")
    prompt_spec = P("dp", "resp", "tensor")
    return jax.shard_map(
        local,
        mesh=mesh,
        in_specs=(token_spec,) * 3 + (prompt_spec,) * 2 + (P(), P(), token_spec)
        + (P("dp", "resp"), P("dp", "resp"), P("dp")),
        out_specs=(token_spec,) * 3 + (prompt_spec,) * 2 + (P(), P()),
        check_vma=False,
    )
```

```python
import functools
import math

import jax
import jax.numpy as jnp
import numpy as np
from jax import lax
from jax.experimental import pallas as pl
from jax.experimental.pallas import tpu as pltpu
from jax.sharding import PartitionSpec as P

EPSILON = 1e-06
THETA = 1000000.0
LOG2_E = math.log2(math.e)
F32, BF16 = jnp.float32, jnp.bfloat16
SMEM = pl.BlockSpec(memory_space=pltpu.SMEM)
VMEM = pl.BlockSpec(memory_space=pltpu.VMEM)
CONTRACT_LAST = (((1,), (1,)), ((), ()))
CONTRACT_FIRST = (((0,), (0,)), ((), ()))
HEADS_AT_ONCE = 2
STEP = 16
UNROLL = 2


def rope_tables(positions, width):
    half = width // 2
    inv_freq = (THETA ** (-(np.arange(half) * 2.0) / width)).astype(np.float32)
    rows = [np.arange(STEP), np.arange(0, positions, STEP)]
    angles = [r[:, None].astype(np.float64) * inv_freq for r in rows]
    sign = np.repeat([-1.0, 1.0], half)
    found = []
    for angle in angles:
        angle = np.concatenate([angle, angle], axis=1)
        found += [np.cos(angle), np.sin(angle) * sign]
    return np.concatenate(found, axis=0).astype(np.float32)


def add_angles(one, other):
    return one[0] * other[0] - one[1] * other[1], one[1] * other[0] + one[0] * other[1]


def rope_at(table_ref, start, count):
    steps = (table_ref.shape[0] - 2 * STEP) // 2
    low = (table_ref[:STEP, :], table_ref[STEP : 2 * STEP, :])

    def high(m):
        first = 2 * STEP + m
        return table_ref[pl.ds(first, 1), :], table_ref[pl.ds(first + steps, 1), :]

    if not isinstance(start, int):
        within = start % STEP
        row = (table_ref[pl.ds(within, 1), :], table_ref[pl.ds(STEP + within, 1), :])
        low = add_angles(low, add_angles(high(start // STEP), row))
    blocks = [add_angles(low, high(m)) for m in range(count // STEP)]
    return tuple(jnp.concatenate([block[i] for block in blocks], axis=0) for i in range(2))


def half_turn(rows):
    return pltpu.roll(rows, rows.shape[1] // 2, 1)


def unit_rows(raw):
    raw = raw.astype(F32)
    inverse = lax.rsqrt(jnp.mean(raw * raw, axis=1, keepdims=True) + EPSILON)
    return raw * inverse, inverse


def rotated(unit, gain, cos, sin):
    normed = unit * gain
    return (normed * cos + half_turn(normed) * sin).astype(BF16)


def rope_back(grad, cos, sin):
    return grad * cos - half_turn(grad) * sin


def norm_back(normed_grad, term, unit, inverse, gain):
    mean = jnp.mean(term * gain, axis=1, keepdims=True)
    return inverse * (normed_grad * gain - unit * mean)


def norm_rope_back(grad, unit, inverse, gain, cos, sin):
    normed_grad = rope_back(grad, cos, sin)
    term = normed_grad * unit
    return norm_back(normed_grad, term, unit, inverse, gain), term


def fold(rows):
    return jnp.sum(rows.reshape(-1, 8, rows.shape[1]), axis=0)


def split_terms(value, terms):
    found = []
    for _ in range(terms):
        found.append(value.astype(BF16).astype(F32))
        value = value - found[-1]
    return found


def send_prompt(key_ref, value_ref, out_ref):
    own = key_ref.shape[0]
    slot = jnp.concatenate([key_ref[...], value_ref[...]], axis=1).astype(F32)
    slots = jnp.concatenate([slot, slot], axis=0).astype(BF16)
    for i in range(out_ref.shape[0] // (2 * own)):
        out_ref[2 * own * i : 2 * own * (i + 1), :] = slots


def head_slices(first, width):
    return [
        pl.ds(pl.multiple_of((first + i) * width, width), width) for i in range(HEADS_AT_ONCE)
    ]


def prepare(
    prompt_len_ref, query_ref, key_ref, query_gain_ref, key_gain_ref, table_ref,
    query_out, key_out, unit_out, shared_out,
):
    length, width = query_ref.shape[0], query_gain_ref.shape[1]
    cos, sin = rope_at(table_ref, prompt_len_ref[0], length)
    shared_out[: table_ref.shape[0], :] = table_ref[...]
    shared_out[table_ref.shape[0] :, :] = jnp.concatenate(
        [query_gain_ref[...], key_gain_ref[...], jnp.zeros((6, width), F32)], axis=0
    )
    for source, gain_ref, out in (
        (key_ref, key_gain_ref, key_out),
        (query_ref, query_gain_ref, query_out),
    ):
        gain = gain_ref[...]

        def one(h, _, source=source, gain=gain, out=out):
            cols = pl.ds(pl.multiple_of(h * width, width), width)
            unit = unit_rows(source[:, cols])[0]
            if out is query_out:
                unit_out[:, cols] = unit.astype(BF16)
            rows = rotated(unit, gain, cos, sin)
            out[pl.ds(pl.multiple_of(h * length, length), length), :] = rows
            return 0

        lax.fori_loop(0, source.shape[1] // width, one, 0, unroll=2)


def attend(
    reward_ref, resp_len_ref, prompt_len_ref,
    arrived_ref, query_ref, key_ref, unit_ref, shared_ref, raw_key_ref, value_ref, grad_ref,
    query_hbm, last_out, key_out, value_out, blocks_out,
    keys, values, key_sum, value_sum, query_terms, key_terms, query_out, sems, *, responses,
):
    length, width = grad_ref.shape[0], shared_ref.shape[1]
    prefix = arrived_ref.shape[0]
    kv_heads = raw_key_ref.shape[1] // width
    kv_cols = kv_heads * width
    group = grad_ref.shape[1] // kv_cols
    own = prefix // responses
    count = HEADS_AT_ONCE * length
    scale = width**-0.5
    start = prompt_len_ref[0]
    table_ref = shared_ref.at[: shared_ref.shape[0] - 8]
    key_gain = shared_ref[pl.ds(shared_ref.shape[0] - 7, 1), :]
    back_cos, back_sin = (t * scale for t in rope_at(table_ref, start, length))
    pre_cos, pre_sin = rope_at(table_ref, 0, prefix)

    valid = lax.broadcasted_iota(jnp.int32, (1, count), 1) % length < resp_len_ref[0, 0]
    visible = (lax.broadcasted_iota(jnp.int32, (prefix, 1), 0) < start).astype(F32)
    causal = lax.broadcasted_iota(jnp.int32, (length, count), 0) <= (
        lax.broadcasted_iota(jnp.int32, (length, count), 1) % length
    )
    query_terms[...] = jnp.zeros_like(query_terms)
    key_terms[...] = jnp.zeros_like(key_terms)

    steps = group // HEADS_AT_ONCE
    step_cols = HEADS_AT_ONCE * width

    def query_copy(c, p):
        source = pl.ds(pl.multiple_of((c * steps + p) * step_cols, step_cols), step_cols)
        target = pl.ds(pl.multiple_of((c * (steps - 1) + p) * step_cols, step_cols), step_cols)
        return pltpu.make_async_copy(
            query_out.at[:, source], query_hbm.at[:, target], sems.at[c * (steps - 1) + p]
        )

    units = []
    for c in range(kv_heads):
        unit = unit_rows(arrived_ref[:, c * width : (c + 1) * width])
        units.append(unit)
        keys[c, :prefix, :] = rotated(unit[0], key_gain, pre_cos, pre_sin)
        keys[c, prefix:, :] = key_ref[c * length : (c + 1) * length, :]
        values[c, :prefix, :] = arrived_ref[:, kv_cols + c * width : kv_cols + (c + 1) * width]
        values[c, prefix:, :] = value_ref[:, c * width : (c + 1) * width]
    key_sum[...] = jnp.zeros_like(key_sum)
    value_sum[...] = jnp.zeros_like(value_sum)

    def products(c, first):
        span = pl.ds(pl.multiple_of(first * length, length), count)
        query_rows = query_ref[span, :]
        grad_rows = jnp.concatenate(
            [grad_ref[:, cols] for cols in head_slices(first, width)], axis=0
        )
        score = lax.dot_general(keys[c], query_rows, CONTRACT_LAST, preferred_element_type=F32)
        dprob = lax.dot_general(values[c], grad_rows, CONTRACT_LAST, preferred_element_type=F32)
        return query_rows, grad_rows, score, dprob

    def softmax(score, dprob):
        expo = jnp.exp2(score * (scale * LOG2_E))
        expo = jnp.concatenate(
            [expo[:prefix] * visible, jnp.where(causal, expo[prefix:], 0.0)], axis=0
        )
        inverse_sum = 1.0 / jnp.sum(expo, axis=0, keepdims=True)
        delta = jnp.sum(expo * dprob, axis=0, keepdims=True) * inverse_sum
        prob = expo * jnp.where(valid, inverse_sum, 0.0)
        return prob.astype(BF16), (prob * (dprob - delta)).astype(BF16)

    def some_heads(p, _):
        firsts = [c * group + p * HEADS_AT_ONCE for c in range(kv_heads)]
        blocks = [products(c, first) for c, first in enumerate(firsts)]
        probs = [softmax(*block[2:]) for block in blocks]
        query_grads = []
        for c, (prob, dscore) in enumerate(probs):
            query_rows, grad_rows = blocks[c][:2]
            key_sum[c] += jnp.dot(dscore, query_rows, preferred_element_type=F32)
            value_sum[c] += jnp.dot(prob, grad_rows, preferred_element_type=F32)
            query_grads.append(
                lax.dot_general(dscore, keys[c], CONTRACT_FIRST, preferred_element_type=F32)
            )
        for c, (first, query_grad) in enumerate(zip(firsts, query_grads)):
            for i, cols in enumerate(head_slices(first, width)):
                normed_grad = rope_back(
                    query_grad[i * length : (i + 1) * length], back_cos, back_sin
                )
                query_out[:, cols] = normed_grad
                query_terms[...] += fold(normed_grad * unit_ref[:, cols].astype(F32))

            @pl.when(p < steps - 1)
            def _(c=c):
                query_copy(c, p).start()

        return 0

    lax.fori_loop(0, steps, some_heads, 0, unroll=UNROLL)
    for c in range(kv_heads):
        own_cols = slice(c * width, (c + 1) * width)
        normed_grad = rope_back(key_sum[c, prefix:, :], back_cos, back_sin)
        key_out[:, own_cols] = normed_grad
        value_out[:, own_cols] = value_sum[c, prefix:, :]
        key_terms[...] += fold(normed_grad * unit_rows(raw_key_ref[:, own_cols])[0])
    for c in range(kv_heads):
        cols = slice(((c + 1) * steps - 1) * step_cols, (c + 1) * steps * step_cols)
        last_out[:, c * step_cols : (c + 1) * step_cols] = query_out[:, cols]
    for c in range(kv_heads):
        raw_grad, term = norm_rope_back(
            key_sum[c, :prefix, :], *units[c], key_gain, pre_cos * scale, pre_sin * scale
        )
        blocks_out[:, c * width : (c + 1) * width] = raw_grad.astype(BF16)
        blocks_out[:, kv_cols + c * width : kv_cols + (c + 1) * width] = value_sum[
            c, :prefix, :
        ].astype(BF16)
        key_terms[...] += fold(term)
    reward = jnp.full((1, width), reward_ref[0, 0], F32)
    rows = split_terms(jnp.sum(query_terms[...], axis=0, keepdims=True), 2)
    rows += split_terms(jnp.sum(key_terms[...], axis=0, keepdims=True), 2)
    rows += split_terms(reward, 3)
    rows = jnp.concatenate(rows + [jnp.zeros((own - len(rows), width), F32)], axis=0)
    pair = jnp.concatenate([rows, rows], axis=0).astype(BF16)
    for i in range(responses // 2):
        blocks_out[2 * own * i : 2 * own * (i + 1), 2 * kv_cols :] = pair
    for c in range(kv_heads):
        for p in range(steps - 1):
            query_copy(c, p).wait()


def advantages(tail, responses):
    tail = tail.astype(F32).reshape(responses, -1, tail.shape[1])
    row = lax.broadcasted_iota(jnp.int32, tail.shape, 1)
    reward = jnp.sum(jnp.where((row >= 4) & (row < 7), tail, 0.0), axis=1, keepdims=True)
    mean = jnp.sum(reward, axis=0, keepdims=True) / responses
    return tail, jnp.broadcast_to(reward - mean, tail.shape), mean[0]


def weigh(blocks_ref, gains_out, *, responses):
    width = gains_out.shape[1]
    tail, weights, _ = advantages(blocks_ref[:, blocks_ref.shape[1] - width :], responses)
    terms = jnp.sum(tail * weights, axis=0)
    query, key = terms[0:1] + terms[1:2], terms[2:3] + terms[3:4]
    row = lax.broadcasted_iota(jnp.int32, gains_out.shape, 0)
    gains_out[...] = jnp.where(row % 2 == 0, query, key)


def finish(
    reward_ref, blocks_ref, raw_query_ref, raw_key_ref, query_gain_ref, key_gain_ref,
    query_ref, last_ref, key_ref, value_ref,
    query_out, key_out, value_out, prefix_key_out, prefix_value_out, *, responses,
):
    own, kv_cols = prefix_key_out.shape
    width = blocks_ref.shape[1] - 2 * kv_cols
    _, weights, mean = advantages(blocks_ref[:, 2 * kv_cols :], responses)
    for out, first in ((prefix_key_out, 0), (prefix_value_out, kv_cols)):
        for cols in range(0, kv_cols, width):
            block = blocks_ref[:, first + cols : first + cols + width].astype(F32)
            out[:, cols : cols + width] = jnp.sum(block.reshape(weights.shape) * weights, axis=0)
    weight = (reward_ref[0, 0] - mean)[:, :1]
    value_out[...] = (value_ref[...] * weight).astype(BF16)
    for cols in range(0, kv_cols, width):
        normed_grad = key_ref[:, cols : cols + width]
        unit, inverse = unit_rows(raw_key_ref[:, cols : cols + width])
        grad = norm_back(normed_grad, normed_grad * unit, unit, inverse, key_gain_ref[...])
        key_out[:, cols : cols + width] = (grad * weight).astype(BF16)
    kv_heads = kv_cols // width
    early, late = query_ref.shape[1] // kv_heads, last_ref.shape[1] // kv_heads
    for c in range(kv_heads):
        first = c * (early + late)
        for source, begin, cols in ((query_ref, first, early), (last_ref, first + early, late)):

            def one(h, _, source=source, begin=begin, skip=c * cols):
                at = [pl.ds(pl.multiple_of(x + h * width, width), width) for x in (begin, skip)]
                normed_grad = source[:, at[1]]
                unit, inverse = unit_rows(raw_query_ref[:, at[0]])
                grad = norm_back(
                    normed_grad, normed_grad * unit, unit, inverse, query_gain_ref[...]
                )
                query_out[:, at[0]] = (grad * weight).astype(BF16)
                return 0

            lax.fori_loop(0, cols // width, one, 0, unroll=2)


def local(
    query_raw, response_key_input, response_value_input, prompt_key_input, prompt_value_input,
    query_gain, key_gain, grad_out, rewards, resp_len, prompt_len,
):
    length = query_raw.shape[2]
    width = query_gain.shape[0]
    kv_cols = response_key_input.shape[3]
    kv_heads = kv_cols // width
    query_heads = query_raw.shape[3] // width
    responses = lax.axis_size("resp")
    own = prompt_key_input.shape[1]
    prefix = own * responses
    slot_cols = 2 * kv_cols + width
    table = jnp.asarray(rope_tables(prefix + length, width))
    gains = (query_gain.reshape(1, width), key_gain.reshape(1, width))
    query, key, value, grad = (
        a[0, 0] for a in (query_raw, response_key_input, response_value_input, grad_out)
    )
    shape = jax.ShapeDtypeStruct

    slots = pl.pallas_call(
        send_prompt,
        out_shape=pltpu.VMEM((prefix, 2 * kv_cols), BF16),
        in_specs=[VMEM] * 2,
        out_specs=VMEM,
        name="send_prompt",
    )(prompt_key_input[0], prompt_value_input[0])
    arrived = lax.all_to_all(slots.reshape(responses, own, 2 * kv_cols), "resp", 0, 0)
    prepared = pl.pallas_call(
        prepare,
        out_shape=(
            pltpu.VMEM((query_heads * length, width), BF16),
            pltpu.VMEM((kv_heads * length, width), BF16),
            pltpu.VMEM(query.shape, BF16),
            pltpu.VMEM((table.shape[0] + 8, width), F32),
        ),
        in_specs=[SMEM] + [VMEM] * 5,
        out_specs=(VMEM,) * 4,
        cost_estimate=pl.CostEstimate(
            flops=100_000_000, bytes_accessed=4_000_000, transcendentals=0
        ),
        name="prepare",
    )(prompt_len, query, key, *gains, table)
    last_cols = kv_heads * HEADS_AT_ONCE * width
    *grads, blocks = pl.pallas_call(
        functools.partial(attend, responses=responses),
        out_shape=(
            pltpu.HBM((length, query.shape[1] - last_cols), F32),
            pltpu.VMEM((length, last_cols), F32),
            pltpu.VMEM(key.shape, F32),
            pltpu.VMEM(key.shape, F32),
            pltpu.VMEM((prefix, slot_cols), BF16),
        ),
        in_specs=[SMEM] * 3 + [VMEM] * 8,
        out_specs=(pl.BlockSpec(memory_space=pltpu.HBM),) + (VMEM,) * 4,
        scratch_shapes=[
            pltpu.VMEM((kv_heads, prefix + length, width), BF16),
            pltpu.VMEM((kv_heads, prefix + length, width), BF16),
            pltpu.VMEM((kv_heads, prefix + length, width), F32),
            pltpu.VMEM((kv_heads, prefix + length, width), F32),
            pltpu.VMEM((8, width), F32),
            pltpu.VMEM((8, width), F32),
            pltpu.VMEM(query.shape, F32),
            pltpu.SemaphoreType.DMA((query_heads // HEADS_AT_ONCE - kv_heads,)),
        ],
        compiler_params=pltpu.CompilerParams(vmem_limit_bytes=16 * 2**20),
        name="attend",
    )(
        rewards, resp_len, prompt_len, arrived.reshape(prefix, 2 * kv_cols), *prepared,
        key, value, grad,
    )
    received = lax.all_to_all(blocks.reshape(responses, own, slot_cols), "resp", 0, 0)
    received = pltpu.with_memory_space_constraint(
        received.reshape(prefix, slot_cols), pltpu.VMEM
    )
    others = lax.axis_size("dp") * lax.axis_size("tensor")
    gain_slots = pl.pallas_call(
        functools.partial(weigh, responses=responses),
        out_shape=pltpu.VMEM((others * 2, width), F32),
        in_specs=[VMEM],
        out_specs=VMEM,
        name="weigh",
    )(received)
    gain_slots = lax.all_to_all(gain_slots.reshape(others, 2, width), ("dp", "tensor"), 0, 0)
    grad_query, grad_key, grad_value, prefix_key, prefix_value = pl.pallas_call(
        functools.partial(finish, responses=responses),
        out_shape=(
            shape(query.shape, BF16),
            shape(key.shape, BF16),
            shape(key.shape, BF16),
            shape((own, kv_cols), F32),
            shape((own, kv_cols), F32),
        ),
        in_specs=[SMEM] + [VMEM] * 9,
        out_specs=(VMEM,) * 5,
        cost_estimate=pl.CostEstimate(
            flops=10_000_000, bytes_accessed=4_000_000, transcendentals=0
        ),
        name="finish",
    )(rewards, received, query, key, *gains, *grads)
    totals = jnp.sum(gain_slots, axis=0) / (lax.axis_size("dp") * responses)
    return (
        grad_query[None, None],
        grad_key[None, None],
        grad_value[None, None],
        prefix_key[None],
        prefix_value[None],
        totals[0],
        totals[1],
    )


def solution(mesh):
    token_spec = P("dp", "resp", None, "tensor")
    prompt_spec = P("dp", "resp", "tensor")
    return jax.shard_map(
        local,
        mesh=mesh,
        in_specs=(token_spec,) * 3 + (prompt_spec,) * 2 + (P(), P(), token_spec)
        + (P("dp", "resp"), P("dp", "resp"), P("dp")),
        out_specs=(token_spec,) * 3 + (prompt_spec,) * 2 + (P(), P()),
        check_vma=False,
    )
```

```python
import functools
import math

import jax
import jax.numpy as jnp
import numpy as np
from jax import lax
from jax.experimental import pallas as pl
from jax.experimental.pallas import tpu as pltpu
from jax.sharding import PartitionSpec as P

EPSILON = 1e-06
THETA = 1000000.0
LOG2_E = math.log2(math.e)
F32, BF16 = jnp.float32, jnp.bfloat16
SMEM = pl.BlockSpec(memory_space=pltpu.SMEM)
VMEM = pl.BlockSpec(memory_space=pltpu.VMEM)
CONTRACT_LAST = (((1,), (1,)), ((), ()))
CONTRACT_FIRST = (((0,), (0,)), ((), ()))
HEADS_AT_ONCE = 2
STEP = 16
UNROLL = 2


def rope_tables(positions, width):
    half = width // 2
    inv_freq = (THETA ** (-(np.arange(half) * 2.0) / width)).astype(np.float32)
    rows = [np.arange(STEP), np.arange(0, positions, STEP)]
    angles = [r[:, None].astype(np.float64) * inv_freq for r in rows]
    sign = np.repeat([-1.0, 1.0], half)
    found = []
    for angle in angles:
        angle = np.concatenate([angle, angle], axis=1)
        found += [np.cos(angle), np.sin(angle) * sign]
    return np.concatenate(found, axis=0).astype(np.float32)


def add_angles(one, other):
    return one[0] * other[0] - one[1] * other[1], one[1] * other[0] + one[0] * other[1]


def rope_at(table_ref, start, count):
    steps = (table_ref.shape[0] - 2 * STEP) // 2
    low = (table_ref[:STEP, :], table_ref[STEP : 2 * STEP, :])

    def high(m):
        first = 2 * STEP + m
        return table_ref[pl.ds(first, 1), :], table_ref[pl.ds(first + steps, 1), :]

    if not isinstance(start, int):
        within = start % STEP
        row = (table_ref[pl.ds(within, 1), :], table_ref[pl.ds(STEP + within, 1), :])
        low = add_angles(low, add_angles(high(start // STEP), row))
    blocks = [add_angles(low, high(m)) for m in range(count // STEP)]
    return tuple(jnp.concatenate([block[i] for block in blocks], axis=0) for i in range(2))


def half_turn(rows):
    return pltpu.roll(rows, rows.shape[1] // 2, 1)


def unit_rows(raw):
    raw = raw.astype(F32)
    inverse = lax.rsqrt(jnp.mean(raw * raw, axis=1, keepdims=True) + EPSILON)
    return raw * inverse, inverse


def rotated(unit, gain, cos, sin):
    normed = unit * gain
    return (normed * cos + half_turn(normed) * sin).astype(BF16)


def rope_back(grad, cos, sin):
    return grad * cos - half_turn(grad) * sin


def norm_back(normed_grad, term, unit, inverse, gain):
    mean = jnp.mean(term * gain, axis=1, keepdims=True)
    return inverse * (normed_grad * gain - unit * mean)


def norm_rope_back(grad, unit, inverse, gain, cos, sin):
    normed_grad = rope_back(grad, cos, sin)
    term = normed_grad * unit
    return norm_back(normed_grad, term, unit, inverse, gain), term


def fold(rows):
    return jnp.sum(rows.reshape(-1, 8, rows.shape[1]), axis=0)


def split_terms(value, terms):
    found = []
    for _ in range(terms):
        found.append(value.astype(BF16).astype(F32))
        value = value - found[-1]
    return found


def send_prompt(key_ref, value_ref, out_ref):
    own = key_ref.shape[0]
    slot = jnp.concatenate([key_ref[...], value_ref[...]], axis=1).astype(F32)
    slots = jnp.concatenate([slot, slot], axis=0).astype(BF16)
    for i in range(out_ref.shape[0] // (2 * own)):
        out_ref[2 * own * i : 2 * own * (i + 1), :] = slots


def head_slices(first, width):
    return [
        pl.ds(pl.multiple_of((first + i) * width, width), width) for i in range(HEADS_AT_ONCE)
    ]


def prepare(
    prompt_len_ref, query_ref, key_ref, query_gain_ref, key_gain_ref, table_ref,
    query_out, key_out, unit_out, shared_out,
):
    length, width = query_ref.shape[0], query_gain_ref.shape[1]
    cos, sin = rope_at(table_ref, prompt_len_ref[0], length)
    shared_out[: table_ref.shape[0], :] = table_ref[...]
    shared_out[table_ref.shape[0] :, :] = jnp.concatenate(
        [query_gain_ref[...], key_gain_ref[...], jnp.zeros((6, width), F32)], axis=0
    )
    for source, gain_ref, out in (
        (key_ref, key_gain_ref, key_out),
        (query_ref, query_gain_ref, query_out),
    ):
        gain = gain_ref[...]

        def one(h, _, source=source, gain=gain, out=out):
            cols = pl.ds(pl.multiple_of(h * width, width), width)
            unit = unit_rows(source[:, cols])[0]
            if out is query_out:
                unit_out[:, cols] = unit.astype(BF16)
            rows = rotated(unit, gain, cos, sin)
            out[pl.ds(pl.multiple_of(h * length, length), length), :] = rows
            return 0

        lax.fori_loop(0, source.shape[1] // width, one, 0, unroll=2)


def attend(
    reward_ref, resp_len_ref, prompt_len_ref,
    arrived_ref, query_ref, key_ref, unit_ref, shared_ref, raw_key_ref, value_ref, grad_ref,
    query_hbm, last_out, key_out, value_out, blocks_out,
    keys, values, key_sum, value_sum, query_terms, key_terms, query_out, sems, *, responses,
):
    length, width = grad_ref.shape[0], shared_ref.shape[1]
    prefix = arrived_ref.shape[0]
    kv_heads = raw_key_ref.shape[1] // width
    kv_cols = kv_heads * width
    group = grad_ref.shape[1] // kv_cols
    own = prefix // responses
    count = HEADS_AT_ONCE * length
    scale = width**-0.5
    start = prompt_len_ref[0]
    table_ref = shared_ref.at[: shared_ref.shape[0] - 8]
    key_gain = shared_ref[pl.ds(shared_ref.shape[0] - 7, 1), :]
    back_cos, back_sin = (t * scale for t in rope_at(table_ref, start, length))
    pre_cos, pre_sin = rope_at(table_ref, 0, prefix)

    valid = lax.broadcasted_iota(jnp.int32, (1, count), 1) % length < resp_len_ref[0, 0]
    visible = (lax.broadcasted_iota(jnp.int32, (prefix, 1), 0) < start).astype(F32)
    causal = lax.broadcasted_iota(jnp.int32, (length, count), 0) <= (
        lax.broadcasted_iota(jnp.int32, (length, count), 1) % length
    )
    query_terms[...] = jnp.zeros_like(query_terms)
    key_terms[...] = jnp.zeros_like(key_terms)

    steps = group // HEADS_AT_ONCE
    step_cols = HEADS_AT_ONCE * width

    def query_copy(c, p):
        source = pl.ds(pl.multiple_of((c * steps + p) * step_cols, step_cols), step_cols)
        target = pl.ds(pl.multiple_of((c * (steps - 1) + p) * step_cols, step_cols), step_cols)
        return pltpu.make_async_copy(
            query_out.at[:, source], query_hbm.at[:, target], sems.at[c * (steps - 1) + p]
        )

    units = []
    for c in range(kv_heads):
        unit = unit_rows(arrived_ref[:, c * width : (c + 1) * width])
        units.append(unit)
        keys[c, :prefix, :] = rotated(unit[0], key_gain, pre_cos, pre_sin)
        keys[c, prefix:, :] = key_ref[c * length : (c + 1) * length, :]
        values[c, :prefix, :] = arrived_ref[:, kv_cols + c * width : kv_cols + (c + 1) * width]
        values[c, prefix:, :] = value_ref[:, c * width : (c + 1) * width]
    key_sum[...] = jnp.zeros_like(key_sum)
    value_sum[...] = jnp.zeros_like(value_sum)

    def products(c, first):
        span = pl.ds(pl.multiple_of(first * length, length), count)
        query_rows = query_ref[span, :]
        grad_rows = jnp.concatenate(
            [grad_ref[:, cols] for cols in head_slices(first, width)], axis=0
        )
        score = lax.dot_general(keys[c], query_rows, CONTRACT_LAST, preferred_element_type=F32)
        dprob = lax.dot_general(values[c], grad_rows, CONTRACT_LAST, preferred_element_type=F32)
        return query_rows, grad_rows, score, dprob

    def softmax(score, dprob):
        expo = jnp.exp2(score * (scale * LOG2_E))
        expo = jnp.concatenate(
            [expo[:prefix] * visible, jnp.where(causal, expo[prefix:], 0.0)], axis=0
        )
        inverse_sum = 1.0 / jnp.sum(expo, axis=0, keepdims=True)
        delta = jnp.sum(expo * dprob, axis=0, keepdims=True) * inverse_sum
        prob = expo * jnp.where(valid, inverse_sum, 0.0)
        return prob.astype(BF16), (prob * (dprob - delta)).astype(BF16)

    def some_heads(p, _):
        firsts = [c * group + p * HEADS_AT_ONCE for c in range(kv_heads)]
        blocks = [products(c, first) for c, first in enumerate(firsts)]
        probs = [softmax(*block[2:]) for block in blocks]
        query_grads = []
        for c, (prob, dscore) in enumerate(probs):
            query_rows, grad_rows = blocks[c][:2]
            key_sum[c] += jnp.dot(dscore, query_rows, preferred_element_type=F32)
            value_sum[c] += jnp.dot(prob, grad_rows, preferred_element_type=F32)
            query_grads.append(
                lax.dot_general(dscore, keys[c], CONTRACT_FIRST, preferred_element_type=F32)
            )
        terms = []
        for c, (first, query_grad) in enumerate(zip(firsts, query_grads)):
            for i, cols in enumerate(head_slices(first, width)):
                normed_grad = rope_back(
                    query_grad[i * length : (i + 1) * length], back_cos, back_sin
                )
                query_out[:, cols] = normed_grad
                terms.append(fold(normed_grad * unit_ref[:, cols].astype(F32)))

            @pl.when(p < steps - 1)
            def _(c=c):
                query_copy(c, p).start()

        query_terms[...] += sum(terms)
        return 0

    lax.fori_loop(0, steps, some_heads, 0, unroll=UNROLL)
    for c in range(kv_heads):
        own_cols = slice(c * width, (c + 1) * width)
        normed_grad = rope_back(key_sum[c, prefix:, :], back_cos, back_sin)
        key_out[:, own_cols] = normed_grad
        value_out[:, own_cols] = value_sum[c, prefix:, :]
        key_terms[...] += fold(normed_grad * unit_rows(raw_key_ref[:, own_cols])[0])
    for c in range(kv_heads):
        cols = slice(((c + 1) * steps - 1) * step_cols, (c + 1) * steps * step_cols)
        last_out[:, c * step_cols : (c + 1) * step_cols] = query_out[:, cols]
    for c in range(kv_heads):
        raw_grad, term = norm_rope_back(
            key_sum[c, :prefix, :], *units[c], key_gain, pre_cos * scale, pre_sin * scale
        )
        blocks_out[:, c * width : (c + 1) * width] = raw_grad.astype(BF16)
        blocks_out[:, kv_cols + c * width : kv_cols + (c + 1) * width] = value_sum[
            c, :prefix, :
        ].astype(BF16)
        key_terms[...] += fold(term)
    reward = jnp.full((1, width), reward_ref[0, 0], F32)
    rows = split_terms(jnp.sum(query_terms[...], axis=0, keepdims=True), 2)
    rows += split_terms(jnp.sum(key_terms[...], axis=0, keepdims=True), 2)
    rows += split_terms(reward, 3)
    rows = jnp.concatenate(rows + [jnp.zeros((own - len(rows), width), F32)], axis=0)
    pair = jnp.concatenate([rows, rows], axis=0).astype(BF16)
    for i in range(responses // 2):
        blocks_out[2 * own * i : 2 * own * (i + 1), 2 * kv_cols :] = pair
    for c in range(kv_heads):
        for p in range(steps - 1):
            query_copy(c, p).wait()


def advantages(tail, responses):
    tail = tail.astype(F32).reshape(responses, -1, tail.shape[1])
    row = lax.broadcasted_iota(jnp.int32, tail.shape, 1)
    reward = jnp.sum(jnp.where((row >= 4) & (row < 7), tail, 0.0), axis=1, keepdims=True)
    mean = jnp.sum(reward, axis=0, keepdims=True) / responses
    return tail, jnp.broadcast_to(reward - mean, tail.shape), mean[0]


def weigh(blocks_ref, gains_out, *, responses):
    width = gains_out.shape[1]
    tail, weights, _ = advantages(blocks_ref[:, blocks_ref.shape[1] - width :], responses)
    terms = jnp.sum(tail * weights, axis=0)
    query, key = terms[0:1] + terms[1:2], terms[2:3] + terms[3:4]
    row = lax.broadcasted_iota(jnp.int32, gains_out.shape, 0)
    gains_out[...] = jnp.where(row % 2 == 0, query, key)


def finish(
    reward_ref, blocks_ref, raw_query_ref, raw_key_ref, query_gain_ref, key_gain_ref,
    query_ref, last_ref, key_ref, value_ref,
    query_out, key_out, value_out, prefix_key_out, prefix_value_out, *, responses,
):
    own, kv_cols = prefix_key_out.shape
    width = blocks_ref.shape[1] - 2 * kv_cols
    _, weights, mean = advantages(blocks_ref[:, 2 * kv_cols :], responses)
    for out, first in ((prefix_key_out, 0), (prefix_value_out, kv_cols)):
        for cols in range(0, kv_cols, width):
            block = blocks_ref[:, first + cols : first + cols + width].astype(F32)
            out[:, cols : cols + width] = jnp.sum(block.reshape(weights.shape) * weights, axis=0)
    weight = (reward_ref[0, 0] - mean)[:, :1]
    value_out[...] = (value_ref[...] * weight).astype(BF16)
    for cols in range(0, kv_cols, width):
        normed_grad = key_ref[:, cols : cols + width]
        unit, inverse = unit_rows(raw_key_ref[:, cols : cols + width])
        grad = norm_back(normed_grad, normed_grad * unit, unit, inverse, key_gain_ref[...])
        key_out[:, cols : cols + width] = (grad * weight).astype(BF16)
    kv_heads = kv_cols // width
    early, late = query_ref.shape[1] // kv_heads, last_ref.shape[1] // kv_heads
    for c in range(kv_heads):
        first = c * (early + late)
        for source, begin, cols in ((query_ref, first, early), (last_ref, first + early, late)):

            def one(h, _, source=source, begin=begin, skip=c * cols):
                at = [pl.ds(pl.multiple_of(x + h * width, width), width) for x in (begin, skip)]
                normed_grad = source[:, at[1]]
                unit, inverse = unit_rows(raw_query_ref[:, at[0]])
                grad = norm_back(
                    normed_grad, normed_grad * unit, unit, inverse, query_gain_ref[...]
                )
                query_out[:, at[0]] = (grad * weight).astype(BF16)
                return 0

            lax.fori_loop(0, cols // width, one, 0, unroll=2)


def local(
    query_raw, response_key_input, response_value_input, prompt_key_input, prompt_value_input,
    query_gain, key_gain, grad_out, rewards, resp_len, prompt_len,
):
    length = query_raw.shape[2]
    width = query_gain.shape[0]
    kv_cols = response_key_input.shape[3]
    kv_heads = kv_cols // width
    query_heads = query_raw.shape[3] // width
    responses = lax.axis_size("resp")
    own = prompt_key_input.shape[1]
    prefix = own * responses
    slot_cols = 2 * kv_cols + width
    table = jnp.asarray(rope_tables(prefix + length, width))
    gains = (query_gain.reshape(1, width), key_gain.reshape(1, width))
    query, key, value, grad = (
        a[0, 0] for a in (query_raw, response_key_input, response_value_input, grad_out)
    )
    shape = jax.ShapeDtypeStruct

    slots = pl.pallas_call(
        send_prompt,
        out_shape=pltpu.VMEM((prefix, 2 * kv_cols), BF16),
        in_specs=[VMEM] * 2,
        out_specs=VMEM,
        name="send_prompt",
    )(prompt_key_input[0], prompt_value_input[0])
    arrived = lax.all_to_all(slots.reshape(responses, own, 2 * kv_cols), "resp", 0, 0)
    prepared = pl.pallas_call(
        prepare,
        out_shape=(
            pltpu.VMEM((query_heads * length, width), BF16),
            pltpu.VMEM((kv_heads * length, width), BF16),
            pltpu.VMEM(query.shape, BF16),
            pltpu.VMEM((table.shape[0] + 8, width), F32),
        ),
        in_specs=[SMEM] + [VMEM] * 5,
        out_specs=(VMEM,) * 4,
        cost_estimate=pl.CostEstimate(
            flops=100_000_000, bytes_accessed=4_000_000, transcendentals=0
        ),
        name="prepare",
    )(prompt_len, query, key, *gains, table)
    last_cols = kv_heads * HEADS_AT_ONCE * width
    *grads, blocks = pl.pallas_call(
        functools.partial(attend, responses=responses),
        out_shape=(
            pltpu.HBM((length, query.shape[1] - last_cols), F32),
            pltpu.VMEM((length, last_cols), F32),
            pltpu.VMEM(key.shape, F32),
            pltpu.VMEM(key.shape, F32),
            pltpu.VMEM((prefix, slot_cols), BF16),
        ),
        in_specs=[SMEM] * 3 + [VMEM] * 8,
        out_specs=(pl.BlockSpec(memory_space=pltpu.HBM),) + (VMEM,) * 4,
        scratch_shapes=[
            pltpu.VMEM((kv_heads, prefix + length, width), BF16),
            pltpu.VMEM((kv_heads, prefix + length, width), BF16),
            pltpu.VMEM((kv_heads, prefix + length, width), F32),
            pltpu.VMEM((kv_heads, prefix + length, width), F32),
            pltpu.VMEM((8, width), F32),
            pltpu.VMEM((8, width), F32),
            pltpu.VMEM(query.shape, F32),
            pltpu.SemaphoreType.DMA((query_heads // HEADS_AT_ONCE - kv_heads,)),
        ],
        compiler_params=pltpu.CompilerParams(vmem_limit_bytes=16 * 2**20),
        name="attend",
    )(
        rewards, resp_len, prompt_len, arrived.reshape(prefix, 2 * kv_cols), *prepared,
        key, value, grad,
    )
    received = lax.all_to_all(blocks.reshape(responses, own, slot_cols), "resp", 0, 0)
    received = pltpu.with_memory_space_constraint(
        received.reshape(prefix, slot_cols), pltpu.VMEM
    )
    others = lax.axis_size("dp") * lax.axis_size("tensor")
    gain_slots = pl.pallas_call(
        functools.partial(weigh, responses=responses),
        out_shape=pltpu.VMEM((others * 2, width), F32),
        in_specs=[VMEM],
        out_specs=VMEM,
        name="weigh",
    )(received)
    gain_slots = lax.all_to_all(gain_slots.reshape(others, 2, width), ("dp", "tensor"), 0, 0)
    grad_query, grad_key, grad_value, prefix_key, prefix_value = pl.pallas_call(
        functools.partial(finish, responses=responses),
        out_shape=(
            shape(query.shape, BF16),
            shape(key.shape, BF16),
            shape(key.shape, BF16),
            shape((own, kv_cols), F32),
            shape((own, kv_cols), F32),
        ),
        in_specs=[SMEM] + [VMEM] * 9,
        out_specs=(VMEM,) * 5,
        cost_estimate=pl.CostEstimate(
            flops=10_000_000, bytes_accessed=4_000_000, transcendentals=0
        ),
        name="finish",
    )(rewards, received, query, key, *gains, *grads)
    totals = jnp.sum(gain_slots, axis=0) / (lax.axis_size("dp") * responses)
    return (
        grad_query[None, None],
        grad_key[None, None],
        grad_value[None, None],
        prefix_key[None],
        prefix_value[None],
        totals[0],
        totals[1],
    )


def solution(mesh):
    token_spec = P("dp", "resp", None, "tensor")
    prompt_spec = P("dp", "resp", "tensor")
    return jax.shard_map(
        local,
        mesh=mesh,
        in_specs=(token_spec,) * 3 + (prompt_spec,) * 2 + (P(), P(), token_spec)
        + (P("dp", "resp"), P("dp", "resp"), P("dp")),
        out_specs=(token_spec,) * 3 + (prompt_spec,) * 2 + (P(), P()),
        check_vma=False,
    )
```
